128 devices in a mesh: src: 8 (over x, core), tgt: 16 (over y, z).
Axes of the slice: x: 4, y: 4, z: 4, core: 2. Of those that a mesh axis runs over, the one named last changes fastest.
Arguments:
- omega: bfloat16 [524288, 128], P(('src', 'tgt')), may hold values from -6 to 6
- owners: int32 [524288, 1], P(('src', 'tgt')), may hold values from 0 to 127; in each aligned block of 4096 rows (0 to 4095, 4096 to 8191, ...) at most 64 rows name the same one
- columns: int32 [524288], P(('src', 'tgt')), may hold values from 0 to 24575
- impedance: float32 [24576], P('tgt'), may hold values from 0.5 to 2
- level_maps: bfloat16 [8, 4, 128, 128], P('src'), may hold values from -0.5 to 0.5
Outputs:
- bases: float32 [8, 24576, 128], P('src', 'tgt')
The draws below stay inside these ranges and needn't reach their ends.
Inputs may be any that keep to these rules, and one draw needn't show every extreme that they name: `owners`: among the 4096 sampled columns of one device no owner is named more than 64 times, a bound that some block reaches.
All inputs are finite; a program needn't handle non-finite values.
Results may differ from the reference program's by a relative error of at most 0.0035.
Values may be sent and summed in bfloat16 or wider, within the bound.
A program may use at most 128 MiB of HBM per device.

```python
import math
import jax
import jax.numpy as jnp
import numpy as np
from jax import lax

RANK = 64
LEVELS = 3
ROWS = 1536
SMP = 4096
NT = 24576
SAMPLES = 524288
CAP = 64
N_SRC = 8
N_TGT = 16


def plant(array, stream_key, low, top_value):
    longest = array.shape.index(max(array.shape))
    spots = []
    for shift in (0, 1):
        where = [jax.random.randint(jax.random.fold_in(stream_key, axis), (), 0, length) for axis, length in enumerate(array.shape)]
        where[longest] = (where[longest] + shift) % array.shape[longest]
        spots.append(tuple(where))
    return array.at[spots[0]].set(low).at[spots[1]].set(top_value)


def block_scale(rng, shape, pieces, least, top_value):
    gain = 1.0
    for axis_at, shards_of in pieces:
        heights = jax.random.uniform(jax.random.fold_in(jax.random.fold_in(rng, 6), axis_at), (shards_of,), jnp.float32, least / len(pieces), top_value / len(pieces))
        gain = gain * jnp.repeat(jnp.exp(heights), shape[axis_at] // shards_of).reshape((-1,) + (1,) * (len(shape) - 1 - axis_at))
    return gain


def assign_block(stream_key, own, number, rows, count, top, limit, skew):
    order = jax.random.permutation(stream_key, count)
    crowded, usual = portions_of(count, rows * top, limit, skew, True), portions_of(count, rows * top, limit, skew, False)
    places = jnp.arange(count)

    def named(sizes, offset_by):
        used = int((sizes > 0).sum())
        fixed = max(1, used // 4)
        moved = fixed + (places - fixed + offset_by * (used - fixed)) % max(1, count - fixed)
        return jnp.zeros((count,), jnp.int32).at[order[jnp.where(places < fixed, places, moved)]].set(jnp.asarray(sizes, jnp.int32))

    sizes = jnp.where(number % 4 == 0, named(crowded, number // 4), named(usual, number - number // 4 - 1))
    mixed = jax.random.permutation(jax.random.fold_in(own, 3), count)
    donor, receiver = mixed[0:count // 2 * 2:2], mixed[1:count // 2 * 2:2]
    room = jnp.minimum(sizes[donor] - 1, limit - sizes[receiver]) // 2
    room = jnp.where((donor == order[0]) | (receiver == order[0]) | (sizes[receiver] == 0), 0, jnp.maximum(room, 0))
    moved = jax.random.randint(jax.random.fold_in(own, 4), (count // 2,), 0, 1 << 20) % (room + 1)
    sizes = sizes.at[donor].add(-moved).at[receiver].add(moved)
    members = jnp.searchsorted(jnp.cumsum(sizes), jnp.arange(rows * top), side="right").astype(jnp.int32)
    listing = members.reshape(top, rows).T
    listing = listing[jax.random.permutation(jax.random.fold_in(own, 1), rows)]
    offset_by = jax.random.randint(jax.random.fold_in(own, 2), (rows, 1), 0, top)
    return jnp.take_along_axis(listing, (jnp.arange(top)[None, :] + offset_by) % top, axis=1)


def portions_of(count, total, limit, lean, full):
    portions = [(1 << 20) // math.isqrt(standing ** lean) + 1 for standing in range(1, count + 1)]
    largest = limit if full else min(limit, max(-(-total // count), total * portions[0] // sum(portions)))
    least = 1 if total - largest >= count - 1 else 0
    given, rest = [largest] + [least] * (count - 1), total - largest - least * (count - 1)
    while rest > 0:
        free = [i for i in range(1, count) if given[i] < largest] or [i for i in range(1, count) if given[i] < limit]
        mass, budget = sum([portions[i] for i in free]), rest
        for i in free:
            extra = min(limit - given[i], max(1, budget * portions[i] // mass), rest)
            given[i] = given[i] + extra
            rest = rest - extra
    return np.array(given)


def scatter_about(own_key, shape, width, bound, pieces=(), kind=jnp.bfloat16):
    values = width * jax.random.normal(own_key, shape, jnp.float32)
    if pieces:
        values = values * block_scale(own_key, shape, pieces, -0.22, 0.18)
    return jnp.clip(values, -bound, bound).astype(kind)


def setup_inputs(seed: int = 0) -> dict:
    streams_of = jax.random.split(jax.random.key(seed), 6)
    omega = scatter_about(streams_of[0], (SAMPLES, 2 * RANK), 1.0, 6.0, ((0, 128),))
    owners_keys = jax.random.split(jax.random.fold_in(streams_of[1], 1), SAMPLES // SMP)
    owners_turns = jax.random.permutation(jax.random.fold_in(streams_of[1], 3), SAMPLES // SMP)
    owners = jax.vmap(lambda own, number: assign_block(jax.random.fold_in(streams_of[1], 2), own, number, SMP, N_SRC * N_TGT, 1, CAP, 2))(owners_keys, owners_turns).reshape((SAMPLES, 1))
    columns = plant(jax.random.randint(streams_of[2], (SAMPLES,), 0, NT), jax.random.fold_in(streams_of[2], 1), 0, NT - 1).astype(jnp.int32)
    impedance = jnp.clip(jnp.exp(math.log(2.0) - 1.3862944 * jax.random.uniform(streams_of[3], (NT,), jnp.float32) ** block_scale(streams_of[3], (NT,), ((0, 16),), -0.2, 0.2)), 0.5, 2.0)
    level_maps = scatter_about(streams_of[4], (N_SRC, LEVELS + 1, 2 * RANK, 2 * RANK), (2 * RANK) ** -0.5, 0.5, ((0, 8),))
    return {"omega": omega, "owners": owners, "columns": columns, "impedance": impedance, "level_maps": level_maps}


highest = lax.Precision.HIGHEST

def node_points(node_index, node_count):
    angles = 2.0 * math.pi / node_count * (node_index.astype(jnp.float32) + 0.5)
    radius = 1.0 + 0.25 * jnp.cos(3.0 * angles)
    return (radius * jnp.cos(angles), radius * jnp.sin(angles))

def sketch_rows(row_first, impedance_rows, column_ids, omega_rows, node_count):
    row_count = impedance_rows.shape[0]
    row_block = min(512, row_count)
    column_block = column_ids.shape[0] // 4
    half_width = omega_rows.shape[1] // 2
    wavenum = node_count / 16.0
    col_x, col_y = node_points(column_ids, node_count)

    def one_block(block_start):
        local_imp = lax.dynamic_slice_in_dim(impedance_rows, block_start, row_block)
        row_ids = row_first + block_start + jnp.arange(row_block, dtype=jnp.int32)
        row_x, row_y = node_points(row_ids, node_count)
        running = jnp.zeros((row_block, omega_rows.shape[1]), jnp.float32)
        for part_index in range(4):
            col_first = part_index * column_block
            delta_x = row_x[:, None] - col_x[None, col_first:col_first + column_block]
            delta_y = row_y[:, None] - col_y[None, col_first:col_first + column_block]
            phases = wavenum * jnp.sqrt(delta_x * delta_x + delta_y * delta_y)
            amplitude = local_imp[:, None] / jnp.sqrt(1.0 + phases)
            real_kernel = (amplitude * jnp.cos(phases)).astype(jnp.bfloat16)
            imag_kernel = (amplitude * jnp.sin(phases)).astype(jnp.bfloat16)
            weights = omega_rows[col_first:col_first + column_block]
            plain_part = jnp.dot(real_kernel.astype(jnp.float32), weights.astype(jnp.float32), preferred_element_type=jnp.float32)
            crossed = jnp.dot(imag_kernel.astype(jnp.float32), weights.astype(jnp.float32), preferred_element_type=jnp.float32)
            running = running + plain_part + jnp.concatenate([-crossed[:, half_width:], crossed[:, :half_width]], axis=1)
        return running
    starts = jnp.arange(row_count // row_block, dtype=jnp.int32) * row_block
    return lax.map(one_block, starts).reshape(row_count, omega_rows.shape[1])

def shifted_factor(gram_matrix):
    dimension = gram_matrix.shape[0]
    shift_value = 0.25 * jnp.trace(gram_matrix) / dimension + 1e-06
    return jnp.linalg.cholesky(gram_matrix + shift_value * jnp.eye(dimension, dtype=gram_matrix.dtype))

def whiten(gram_matrix, matrix):
    factor = shifted_factor(gram_matrix)
    return lax.linalg.triangular_solve(factor, matrix, left_side=False, lower=True, transpose_a=True)

def reference(omega, owners, columns, impedance, level_maps):
    owner_total = N_SRC * N_TGT
    slot_total = owner_total * CAP
    col_width = 2 * RANK
    owner_grid = owners[:, 0].reshape(owner_total, SMP)

    def sender_ranks(owner_row):
        onehot = (owner_row[:, None] == jnp.arange(owner_total, dtype=jnp.int32)[None, :]).astype(jnp.int32)
        earlier = jnp.cumsum(onehot, axis=0) - onehot
        return lax.optimization_barrier(jnp.sum(earlier * onehot, axis=1))
    slot_rank = lax.map(sender_ranks, owner_grid)
    sender = jnp.arange(owner_total, dtype=jnp.int32)[:, None]
    target_slot = owner_grid * slot_total + sender * CAP + slot_rank
    slot_table = jnp.full((owner_total * slot_total,), owner_total * SMP, jnp.int32)
    slot_table = slot_table.at[target_slot.reshape(-1)].set(jnp.arange(owner_total * SMP, dtype=jnp.int32))
    slot_table = slot_table.reshape(owner_total, slot_total)
    omega_ext = jnp.concatenate([omega, jnp.zeros((1, omega.shape[1]), omega.dtype)], axis=0)
    column_ext = jnp.concatenate([columns, jnp.zeros((1,), jnp.int32)], axis=0)

    def owner_sketch(owner):
        slot_picks = slot_table[owner]
        tgt_box = owner % N_TGT
        imp_rows = lax.dynamic_slice_in_dim(impedance, tgt_box * ROWS, ROWS)
        return sketch_rows(tgt_box * ROWS, imp_rows, column_ext[slot_picks], omega_ext[slot_picks], NT).astype(jnp.bfloat16)
    sketch = lax.map(owner_sketch, jnp.arange(owner_total, dtype=jnp.int32))
    sketch = sketch.reshape(N_SRC, N_TGT, ROWS, col_width).astype(jnp.float32)
    maps_wide = level_maps.astype(jnp.float32)
    mixed_rows = jnp.einsum('stmc,scd->stmd', sketch, maps_wide[:, 0], precision=highest)
    gram_batch = jnp.einsum('stmc,stmd->stcd', mixed_rows, mixed_rows, precision=highest) / ROWS
    basis_rows = jax.vmap(jax.vmap(whiten))(gram_batch, mixed_rows)
    for level_index in range(LEVELS):
        child_span = 2 ** level_index
        mixed_rows = jnp.einsum('stmc,scd->stmd', sketch, maps_wide[:, level_index + 1], precision=highest)
        local_part = jnp.einsum('stmc,stmd->stcd', basis_rows, mixed_rows, precision=highest) / (ROWS * child_span)
        grouped = local_part.reshape(N_SRC, N_TGT // child_span, child_span, col_width, col_width).sum(axis=2)
        swapped = grouped.reshape(N_SRC, N_TGT // (2 * child_span), 2, col_width, col_width)[:, :, ::-1]
        swapped = swapped.reshape(N_SRC, N_TGT // child_span, col_width, col_width)
        own_sum = jnp.repeat(grouped, child_span, axis=1)
        other_sum = jnp.repeat(swapped, child_span, axis=1)
        gram_batch = (jnp.einsum('stca,stcb->stab', own_sum, own_sum, precision=highest) + jnp.einsum('stca,stcb->stab', other_sum, other_sum, precision=highest)) / 2.0
        transfer = jax.vmap(jax.vmap(whiten))(gram_batch, own_sum)
        basis_rows = jnp.einsum('stmc,stcd->stmd', basis_rows, transfer, precision=highest)
    return basis_rows.reshape(N_SRC, NT, col_width)
```

```python
import functools
import math

import jax
import jax.numpy as jnp
from jax import lax
from jax.experimental import pallas as pl
from jax.experimental.pallas import tpu as pltpu
from jax.sharding import PartitionSpec as P

highest = lax.Precision.HIGHEST
SINE = (4.4415356787207045, -7.2646801556685014, 3.252047353220934)
COSINE = (1.414204078817102, -6.977641981219209, 5.715237646584958, -1.728346667500456)


def partner(shard, axis, apart):
    return lax.ppermute(shard, axis, [(i, i ^ 1 << apart) for i in range(lax.axis_size(axis))])


def node_points(node_index, node_count):
    angles = 2.0 * math.pi / node_count * (node_index.astype(jnp.float32) + 0.5)
    radius = 1.0 + 0.25 * jnp.cos(3.0 * angles)
    return (radius * jnp.cos(angles), radius * jnp.sin(angles))


def kernel_block(rows, wide, step, row_x, row_y, col_x, col_y, weights, scale, out, parts):
    @pl.loop(0, rows // step)
    def _(index):
        here = pl.ds(pl.multiple_of(index * step, step), step)
        below = pl.ds(pl.multiple_of(rows + index * step, step), step)
        x, y = row_x[here, :], row_y[here, :]
        for first in range(0, wide, 128):
            lanes = slice(first, first + 128)
            dx = x - col_x[0:1, lanes]
            dy = y - col_y[0:1, lanes]
            square = jnp.maximum(dx * dx + dy * dy, 1e-30)
            turns = square * lax.rsqrt(square)
            part = turns - jnp.round(turns)
            amplitude = lax.rsqrt(turns + 0.5 / math.pi)
            z = part * part
            sine = part * (SINE[0] + z * (SINE[1] + z * SINE[2]))
            cosine = COSINE[0] + z * (COSINE[1] + z * (COSINE[2] + z * COSINE[3]))
            scaled = amplitude * sine
            parts[here, lanes] = (amplitude - scaled * sine).astype(jnp.bfloat16)
            parts[below, lanes] = (scaled * cosine).astype(jnp.bfloat16)

    both = jnp.dot(parts[...], weights[...], preferred_element_type=jnp.float32)
    half = both.shape[1] // 2
    crossed = both[rows:]
    product = both[:rows] + jnp.concatenate([-crossed[:, half:], crossed[:, :half]], axis=1)
    product = product * scale[...]

    @pl.when(pl.program_id(1) == 0)
    def _():
        out[...] = product

    @pl.when(pl.program_id(1) > 0)
    def _():
        out[...] += product


def sketch_rows(row_first, impedance_rows, column_ids, omega_rows, node_count):
    rows, columns = impedance_rows.shape[0], column_ids.shape[0]
    row_block, wide, step = 512, 1024, 32
    width = omega_rows.shape[1]
    turn = node_count / 16.0 / (2.0 * math.pi)
    col_x, col_y = node_points(column_ids, node_count)
    row_x, row_y = node_points(row_first + jnp.arange(rows, dtype=jnp.int32), node_count)
    spread = lambda v: jnp.broadcast_to(v[:, None], (rows, 128))
    row_spec = pl.BlockSpec((row_block, 128), lambda i, j: (i, 0))
    col_spec = pl.BlockSpec((1, wide), lambda i, j: (0, j))
    return pl.pallas_call(
        functools.partial(kernel_block, row_block, wide, step),
        grid=(rows // row_block, columns // wide),
        in_specs=[
            row_spec,
            row_spec,
            col_spec,
            col_spec,
            pl.BlockSpec((wide, width), lambda i, j: (j, 0)),
            row_spec,
        ],
        out_specs=pl.BlockSpec((row_block, width), lambda i, j: (i, 0)),
        out_shape=jax.ShapeDtypeStruct((rows, width), jnp.float32),
        scratch_shapes=[pltpu.VMEM((2 * row_block, wide), jnp.bfloat16)],
        compiler_params=pltpu.CompilerParams(vmem_limit_bytes=40 << 20),
    )(
        spread(row_x * turn),
        spread(row_y * turn),
        (col_x * turn)[None],
        (col_y * turn)[None],
        omega_rows,
        spread(impedance_rows / math.sqrt(2.0 * math.pi)),
    )


def shifted_factor(gram_matrix):
    dimension = gram_matrix.shape[0]
    shift_value = 0.25 * jnp.trace(gram_matrix) / dimension + 1e-06
    return jnp.linalg.cholesky(
        gram_matrix + shift_value * jnp.eye(dimension, dtype=gram_matrix.dtype)
    )


def whiten(gram_matrix, matrix):
    factor = shifted_factor(gram_matrix)
    return lax.linalg.triangular_solve(
        factor, matrix, left_side=False, lower=True, transpose_a=True
    )


def matmul(first_matrix, second_matrix):
    return jnp.dot(first_matrix, second_matrix, precision=highest)


def sketch_mix(sketch, level_map):
    return jnp.dot(sketch, level_map, preferred_element_type=jnp.float32)


def per_device(omega, owners, columns, impedance, level_maps):
    sample_count = omega.shape[0]
    device_count = lax.axis_size(("src", "tgt"))
    tgt_count = lax.axis_size("tgt")
    capacity = 2 * sample_count // device_count
    owner_list = owners[:, 0]
    onehot = (owner_list[:, None] == jnp.arange(device_count, dtype=jnp.int32)[None, :]).astype(
        jnp.int32
    )
    earlier = jnp.cumsum(onehot, axis=0) - onehot
    slot_rank = jnp.sum(earlier * onehot, axis=1)
    position = owner_list * capacity + slot_rank
    send_rows = (
        jnp.zeros((device_count * capacity, omega.shape[1]), omega.dtype).at[position].set(omega)
    )
    send_ids = jnp.zeros((device_count * capacity,), jnp.int32).at[position].set(columns)
    got_rows, got_ids = (
        lax.all_to_all(
            send_rows.reshape(device_count, capacity, omega.shape[1]),
            ("src", "tgt"),
            split_axis=0,
            concat_axis=0,
            tiled=True,
        ),
        lax.all_to_all(
            send_ids.reshape(device_count, capacity),
            ("src", "tgt"),
            split_axis=0,
            concat_axis=0,
            tiled=True,
        ),
    )
    slot_rows = got_rows.reshape(device_count * capacity, omega.shape[1])
    slot_ids = got_ids.reshape(device_count * capacity)
    row_count = impedance.shape[0]
    node_count = tgt_count * row_count
    tgt_place = lax.axis_index("tgt")
    sketch = sketch_rows(tgt_place * row_count, impedance, slot_ids, slot_rows, node_count).astype(
        jnp.bfloat16
    )
    maps_here = level_maps[0]
    level_count = maps_here.shape[0] - 1
    mixed_rows = sketch_mix(sketch, maps_here[0])
    basis_rows = whiten(matmul(mixed_rows.T, mixed_rows) / row_count, mixed_rows)
    for level_index in range(level_count):
        child_span = 2**level_index
        mixed_rows = sketch_mix(sketch, maps_here[level_index + 1])
        local_part = matmul(basis_rows.T, mixed_rows) / (row_count * child_span)
        own_sum = local_part
        for bit_index in range(level_index):
            own_sum = own_sum + partner(own_sum, "tgt", bit_index)
        other_sum = partner(own_sum, "tgt", level_index)
        gram_matrix = (matmul(own_sum.T, own_sum) + matmul(other_sum.T, other_sum)) / 2.0
        basis_rows = matmul(basis_rows, whiten(gram_matrix, own_sum))
    return basis_rows[None]


def solution(mesh):
    in_specs = (
        P(("src", "tgt"), None),
        P(("src", "tgt"), None),
        P(("src", "tgt")),
        P("tgt"),
        P("src", None, None, None),
    )
    out_specs = P("src", "tgt", None)
    return jax.shard_map(
        per_device, mesh=mesh, in_specs=in_specs, out_specs=out_specs, check_vma=False
    )
```

```python
import functools
import math

import jax
import jax.numpy as jnp
from jax import lax
from jax.experimental import pallas as pl
from jax.experimental.pallas import tpu as pltpu
from jax.sharding import PartitionSpec as P

MESH = pl.DeviceIdType.MESH
SINE = (4.4415356787207045, -7.2646801556685014, 3.252047353220934)
COSINE = (1.414204078817102, -6.977641981219209, 5.715237646584958, -1.728346667500456)


def node_points(node_index, node_count):
    angles = 2.0 * math.pi / node_count * (node_index.astype(jnp.float32) + 0.5)
    radius = 1.0 + 0.25 * jnp.cos(3.0 * angles)
    return (radius * jnp.cos(angles), radius * jnp.sin(angles))


def kernel_block(rows, wide, step, row_x, row_y, col_x, col_y, weights, scale, out, parts):
    @pl.loop(0, rows // step)
    def _(index):
        here = pl.ds(pl.multiple_of(index * step, step), step)
        below = pl.ds(pl.multiple_of(rows + index * step, step), step)
        x, y = row_x[here, :], row_y[here, :]
        for first in range(0, wide, 128):
            lanes = slice(first, first + 128)
            dx = x - col_x[0:1, lanes]
            dy = y - col_y[0:1, lanes]
            square = jnp.maximum(dx * dx + dy * dy, 1e-30)
            turns = square * lax.rsqrt(square)
            part = turns - jnp.round(turns)
            amplitude = lax.rsqrt(turns + 0.5 / math.pi)
            z = part * part
            sine = part * (SINE[0] + z * (SINE[1] + z * SINE[2]))
            cosine = COSINE[0] + z * (COSINE[1] + z * (COSINE[2] + z * COSINE[3]))
            scaled = amplitude * sine
            parts[here, lanes] = (amplitude - scaled * sine).astype(jnp.bfloat16)
            parts[below, lanes] = (scaled * cosine).astype(jnp.bfloat16)

    both = jnp.dot(parts[...], weights[...], preferred_element_type=jnp.float32)
    half = both.shape[1] // 2
    crossed = both[rows:]
    product = both[:rows] + jnp.concatenate([-crossed[:, half:], crossed[:, :half]], axis=1)
    product = product * scale[...]

    @pl.when(pl.program_id(1) == 0)
    def _():
        out[...] = product

    @pl.when(pl.program_id(1) > 0)
    def _():
        out[...] += product


def sketch_rows(row_first, impedance_rows, column_ids, omega_rows, node_count):
    rows, columns = impedance_rows.shape[0], column_ids.shape[0]
    row_block, wide, step = 512, 1024, 32
    width = omega_rows.shape[1]
    turn = node_count / 16.0 / (2.0 * math.pi)
    col_x, col_y = node_points(column_ids, node_count)
    row_x, row_y = node_points(row_first + jnp.arange(rows, dtype=jnp.int32), node_count)
    spread = lambda v: jnp.broadcast_to(v[:, None], (rows, 128))
    row_spec = pl.BlockSpec((row_block, 128), lambda i, j: (i, 0))
    col_spec = pl.BlockSpec((1, wide), lambda i, j: (0, j))
    return pl.pallas_call(
        functools.partial(kernel_block, row_block, wide, step),
        grid=(rows // row_block, columns // wide),
        in_specs=[
            row_spec,
            row_spec,
            col_spec,
            col_spec,
            pl.BlockSpec((wide, width), lambda i, j: (j, 0)),
            row_spec,
        ],
        out_specs=pl.BlockSpec((row_block, width), lambda i, j: (i, 0)),
        out_shape=jax.ShapeDtypeStruct((rows, width), jnp.float32),
        scratch_shapes=[pltpu.VMEM((2 * row_block, wide), jnp.bfloat16)],
        compiler_params=pltpu.CompilerParams(vmem_limit_bytes=40 << 20),
    )(
        spread(row_x * turn),
        spread(row_y * turn),
        (col_x * turn)[None],
        (col_y * turn)[None],
        omega_rows,
        spread(impedance_rows / math.sqrt(2.0 * math.pi)),
    )


def split(values, axis, order):
    high = values.astype(jnp.bfloat16)
    rest = values - high.astype(jnp.float32)
    middle = rest.astype(jnp.bfloat16)
    low = (rest - middle.astype(jnp.float32)).astype(jnp.bfloat16)
    pieces = (high, middle, low)
    return jnp.concatenate([pieces[i] for i in order], axis=axis)


LEFT, RIGHT = (0, 0, 1, 0, 1, 2), (0, 1, 0, 2, 1, 0)


def product(first, second, first_axis=1, second_axis=0):
    return lax.dot_general(
        split(first, first_axis, LEFT),
        split(second, second_axis, RIGHT),
        (((first_axis,), (second_axis,)), ((), ())),
        preferred_element_type=jnp.float32,
    )


def spread_rows(row, count):
    return jnp.broadcast_to(row, (count, row.shape[1]))


def eliminate_panel(panel, first, lanes):
    pieces = panel.shape[0] // 8
    rows = [panel[8 * i : 8 * i + 8] for i in range(pieces)]
    sublane = lax.broadcasted_iota(jnp.int32, (8, lanes), 0)
    twice = lambda v: jnp.concatenate([v, v], axis=1)
    done = []
    for top in range(pieces):
        columns = [
            [
                jnp.take_along_axis(
                    rows[i][:, :lanes],
                    jnp.full((8, lanes), first + 8 * top + t, jnp.int32),
                    axis=1,
                )
                for i in range(top, pieces)
            ]
            for t in range(8)
        ]
        for t in range(8):
            pivot = spread_rows(columns[t][0][t : t + 1], 8)
            inverse = 1.0 / pivot
            row = rows[top][t : t + 1]
            done.append(row * twice(lax.rsqrt(pivot[0:1])))
            factors = [c * inverse for c in columns[t]]
            factors[0] = jnp.where(sublane > t, factors[0], 0.0)
            for u in range(t + 1, 8):
                entry = spread_rows(columns[u][0][t : t + 1], 8)
                columns[u] = [c - f * entry for c, f in zip(columns[u], factors)]
            full_row = spread_rows(row, 8)
            for i, f in enumerate(factors):
                rows[top + i] = rows[top + i] - twice(f) * full_row
    return jnp.concatenate(done, axis=0)


def factor_solve(gram_matrix, right):
    size, block = gram_matrix.shape[0], 32
    diagonal = lax.broadcasted_iota(jnp.int32, (size, size), 0) == lax.broadcasted_iota(
        jnp.int32, (size, size), 1
    )
    trace = jnp.sum(jnp.where(diagonal, gram_matrix, 0.0), axis=(0, 1), keepdims=True)
    shifted = gram_matrix + jnp.where(diagonal, 0.25 * trace / size + 1e-06, 0.0)
    rest = jnp.concatenate([shifted, right], axis=1)
    solved = []
    for first in range(0, size, block):
        panel = eliminate_panel(rest[:block], first, size)
        solved.append(panel[:, size:])
        if first + block < size:
            rest = rest[block:] - product(panel[:, :size], panel, 0, 0)[first + block :]
    return jnp.concatenate(solved, axis=0)


def merge_kernel(rows, sketch, maps, out, sends, gots, send_sems, got_sems):
    src, tgt = lax.axis_index("src"), lax.axis_index("tgt")
    mates = (
        tgt + 1 - 2 * (tgt % 2),
        tgt + 2 - 4 * ((tgt // 2) % 2),
        tgt + 3 - 2 * (tgt % 4),
        tgt + 4 - 8 * ((tgt // 4) % 2),
    )
    barrier = pltpu.get_barrier_semaphore()
    for mate in mates:
        pl.semaphore_signal(barrier, inc=1, device_id=(src, mate), device_id_type=MESH)
    pl.semaphore_wait(barrier, len(mates))

    copies = []

    def post(values, targets):
        source = sends.at[sum(len(c) > 0 for c in copies)]
        source[...] = values
        base = sum(len(c) for c in copies)
        batch = []
        for i, target in enumerate(targets):
            copy = pltpu.make_async_remote_copy(
                src_ref=source,
                dst_ref=gots.at[base + i],
                send_sem=send_sems.at[base + i],
                recv_sem=got_sems.at[base + i],
                device_id=(src, mates[target]),
                device_id_type=MESH,
            )
            copy.start()
            batch.append((copy, base + i))
        copies.append(batch)
        return batch

    def take(batch):
        values = []
        for copy, slot in batch:
            copy.wait_recv()
            values.append(gots[slot])
        return values

    cross = lax.dot_general(
        sketch[...], sketch[...], (((0,), (0,)), ((), ())), preferred_element_type=jnp.float32
    )
    wide_maps = [maps[k].astype(jnp.float32) for k in range(4)]
    images = [product(cross, m) for m in wide_maps]
    gram_matrix = product(wide_maps[0], images[0], 0, 0) / rows
    turned = factor_solve(gram_matrix, wide_maps[0].T)
    for level in range(3):
        part = product(turned, images[level + 1]) / (rows * 2**level)
        if level == 0:
            batch = post(part, (0,))
            own = part
        else:
            batch = post(part, (0, 1, 2))
            near, far, beyond = take(batch)
            own = part + near
            if level == 1:
                other = far + beyond
            else:
                own = own + (far + beyond)
                batch = post(own, (3,))
        mine = product(own, own, 0, 0)
        right = product(own, turned, 0, 0)
        if level != 1:
            (other,) = take(batch)
        gram_matrix = (mine + product(other, other, 0, 0)) / 2.0
        turned = factor_solve(gram_matrix, right)
    for batch in copies:
        for copy, _ in batch:
            copy.wait_send()
    turned = split(turned, 1, (0, 1, 2))
    sketch_here = sketch[...]
    out[...] = lax.dot_general(
        jnp.concatenate([sketch_here] * 3, axis=1),
        turned,
        (((1,), (1,)), ((), ())),
        preferred_element_type=jnp.float32,
    )


def merged_bases(sketch, maps_here):
    rows, width = sketch.shape
    tile = (width, width)
    return pl.pallas_call(
        functools.partial(merge_kernel, rows),
        out_shape=jax.ShapeDtypeStruct((rows, width), jnp.float32),
        in_specs=[pl.BlockSpec(memory_space=pltpu.VMEM)] * 2,
        out_specs=pl.BlockSpec(memory_space=pltpu.VMEM),
        scratch_shapes=[
            pltpu.VMEM((4, *tile), jnp.float32),
            pltpu.VMEM((8, *tile), jnp.float32),
            pltpu.SemaphoreType.DMA((8,)),
            pltpu.SemaphoreType.DMA((8,)),
        ],
        compiler_params=pltpu.CompilerParams(
            collective_id=0, has_side_effects=True, vmem_limit_bytes=40 << 20
        ),
    )(sketch, maps_here)


def per_device(omega, owners, columns, impedance, level_maps):
    sample_count = omega.shape[0]
    device_count = lax.axis_size(("src", "tgt"))
    tgt_count = lax.axis_size("tgt")
    capacity = 2 * sample_count // device_count
    owner_list = owners[:, 0]
    onehot = (owner_list[:, None] == jnp.arange(device_count, dtype=jnp.int32)[None, :]).astype(
        jnp.int32
    )
    earlier = jnp.cumsum(onehot, axis=0) - onehot
    slot_rank = jnp.sum(earlier * onehot, axis=1)
    position = owner_list * capacity + slot_rank
    send_rows = (
        jnp.zeros((device_count * capacity, omega.shape[1]), omega.dtype).at[position].set(omega)
    )
    send_ids = jnp.zeros((device_count * capacity,), jnp.int32).at[position].set(columns)
    got_rows, got_ids = (
        lax.all_to_all(
            send_rows.reshape(device_count, capacity, omega.shape[1]),
            ("src", "tgt"),
            split_axis=0,
            concat_axis=0,
            tiled=True,
        ),
        lax.all_to_all(
            send_ids.reshape(device_count, capacity),
            ("src", "tgt"),
            split_axis=0,
            concat_axis=0,
            tiled=True,
        ),
    )
    slot_rows = got_rows.reshape(device_count * capacity, omega.shape[1])
    slot_ids = got_ids.reshape(device_count * capacity)
    row_count = impedance.shape[0]
    node_count = tgt_count * row_count
    tgt_place = lax.axis_index("tgt")
    sketch = sketch_rows(tgt_place * row_count, impedance, slot_ids, slot_rows, node_count).astype(
        jnp.bfloat16
    )
    maps_here = level_maps[0]
    return merged_bases(sketch, maps_here)[None]


def solution(mesh):
    in_specs = (
        P(("src", "tgt"), None),
        P(("src", "tgt"), None),
        P(("src", "tgt")),
        P("tgt"),
        P("src", None, None, None),
    )
    out_specs = P("src", "tgt", None)
    return jax.shard_map(
        per_device, mesh=mesh, in_specs=in_specs, out_specs=out_specs, check_vma=False
    )
```

```python
import functools
import math

import jax
import jax.numpy as jnp
from jax import lax
from jax.experimental import pallas as pl
from jax.experimental.pallas import tpu as pltpu
from jax.sharding import PartitionSpec as P

MESH = pl.DeviceIdType.MESH
SINE = (4.4415356787207045, -7.2646801556685014, 3.252047353220934)
COSINE = (1.414204078817102, -6.977641981219209, 5.715237646584958, -1.728346667500456)


def node_points(node_index, node_count):
    angles = 2.0 * math.pi / node_count * (node_index.astype(jnp.float32) + 0.5)
    radius = 1.0 + 0.25 * jnp.cos(3.0 * angles)
    return (radius * jnp.cos(angles), radius * jnp.sin(angles))


def thirds(values):
    high = values.astype(jnp.bfloat16)
    rest = values - high.astype(jnp.float32)
    middle = rest.astype(jnp.bfloat16)
    low = (rest - middle.astype(jnp.float32)).astype(jnp.bfloat16)
    return high, middle, low


def pack_kernel(
    capacity, owners, col_x, col_y, omega, rows_out, points_out, places, placed, table, wide, plain, sem
):
    blocks, lanes = owners.shape
    count = points_out.shape[0]
    owner_at = lax.broadcasted_iota(jnp.int32, (count, lanes), 0)
    before = (
        lax.broadcasted_iota(jnp.int32, (lanes, lanes), 0)
        < lax.broadcasted_iota(jnp.int32, (lanes, lanes), 1)
    ).astype(jnp.float32).astype(jnp.bfloat16)
    ones = jnp.ones((lanes, lanes), jnp.bfloat16)
    rank_at = lax.broadcasted_iota(jnp.int32, (capacity, lanes), 0)
    wide[...] = jnp.zeros_like(wide)
    table[...] = jnp.zeros_like(table)
    plain[...] = omega[...].astype(jnp.float32)

    def one_block(index, running):
        here = pl.ds(index, 1)
        owner = owners[here, :]
        named = owner_at == owner
        onehot = named.astype(jnp.float32).astype(jnp.bfloat16)
        earlier = jnp.dot(onehot, before, preferred_element_type=jnp.float32) + running
        rank = jnp.sum(jnp.where(named, earlier, 0.0), axis=0, keepdims=True).astype(jnp.int32)
        places[here, :] = owner * capacity + rank
        ranked = rank_at == rank
        pieces = [
            jnp.where(ranked, piece.astype(jnp.float32), 0.0).astype(jnp.bfloat16)
            for values in (col_x[here, :], col_y[here, :])
            for piece in thirds(values)
        ]
        table[...] += lax.dot_general(
            onehot,
            jnp.concatenate(pieces, axis=0),
            (((1,), (1,)), ((), ())),
            preferred_element_type=jnp.float32,
        )
        return running + jnp.dot(onehot, ones, preferred_element_type=jnp.float32)

    lax.fori_loop(0, blocks, one_block, jnp.zeros((count, lanes), jnp.float32), unroll=4)
    copy = pltpu.make_async_copy(places, placed, sem)
    copy.start()
    sums = table[...]
    piece = [sums[:, i * capacity : (i + 1) * capacity] for i in range(6)]
    points_out[...] = jnp.concatenate(
        [(piece[2] + piece[1]) + piece[0], (piece[5] + piece[4]) + piece[3]], axis=1
    )
    copy.wait()

    @pl.loop(0, blocks)
    def _(block):
        @pl.loop(0, lanes // 32)
        def _(part):
            for lane in range(32):
                at = part * 32 + lane
                wide[pl.ds(placed[block, at], 1), :] = plain[pl.ds(block * lanes + at, 1), :]

    rows_out[...] = wide[...].astype(jnp.bfloat16)


def packed_slots(omega, owners, columns, count, node_count):
    samples, width = omega.shape
    lanes = 128
    blocks = samples // lanes
    capacity = 2 * samples // count
    turn = node_count / 16.0 / (2.0 * math.pi)
    col_x, col_y = node_points(columns.reshape(blocks, lanes), node_count)
    vmem = pl.BlockSpec(memory_space=pltpu.VMEM)
    return pl.pallas_call(
        functools.partial(pack_kernel, capacity),
        out_shape=(
            jax.ShapeDtypeStruct((count * capacity, width), jnp.bfloat16),
            jax.ShapeDtypeStruct((count, 2 * capacity), jnp.float32),
        ),
        in_specs=[vmem] * 4,
        out_specs=(vmem, vmem),
        scratch_shapes=[
            pltpu.VMEM((blocks, lanes), jnp.int32),
            pltpu.SMEM((blocks, lanes), jnp.int32),
            pltpu.VMEM((count, 6 * capacity), jnp.float32),
            pltpu.VMEM((count * capacity, width), jnp.float32),
            pltpu.VMEM((samples, width), jnp.float32),
            pltpu.SemaphoreType.DMA,
        ],
        compiler_params=pltpu.CompilerParams(vmem_limit_bytes=40 << 20),
    )(owners.reshape(blocks, lanes), col_x * turn, col_y * turn, omega)


def kernel_values(x, y, col_x, col_y):
    dx = x - col_x
    dy = y - col_y
    square = jnp.maximum(dx * dx + dy * dy, 1e-30)
    turns = square * lax.rsqrt(square)
    part = turns - jnp.round(turns)
    amplitude = lax.rsqrt(turns + 0.5 / math.pi)
    z = part * part
    sine = part * (SINE[0] + z * (SINE[1] + z * SINE[2]))
    cosine = COSINE[0] + z * (COSINE[1] + z * (COSINE[2] + z * COSINE[3]))
    scaled = amplitude * sine
    return (amplitude - scaled * sine).astype(jnp.bfloat16), (scaled * cosine).astype(jnp.bfloat16)


def sketch_kernel(
    shape, slots, points, row_x, row_y, scale, out, got, got_points, cols, parts, total, sent, got_sems
):
    src_count, tgt_count = shape
    src, tgt = lax.axis_index("src"), lax.axis_index("tgt")
    rows, lanes = row_x.shape
    capacity, width = slots.shape[1:]
    chunk, step = 512, 32
    columns = tgt_count * capacity

    def device(offset):
        return (
            (src + offset // tgt_count) % src_count,
            (tgt + offset % tgt_count) % tgt_count,
        )

    barrier = pltpu.get_barrier_semaphore()

    @pl.loop(1, src_count * tgt_count)
    def _(offset):
        pl.semaphore_signal(barrier, inc=1, device_id=device(offset), device_id_type=MESH)

    me = src * tgt_count + tgt
    pltpu.make_async_copy(points.at[me], got_points.at[0, 0], got_sems.at[0, 0]).start()
    pltpu.make_async_copy(slots.at[me], got.at[0, 0], got_sems.at[1, 0]).start()
    pl.semaphore_wait(barrier, src_count * tgt_count - 1)

    @pl.loop(1, src_count * tgt_count)
    def _(offset):
        there = device(offset)
        owner = there[0] * tgt_count + there[1]
        group, place = offset // tgt_count, offset % tgt_count
        for kind, (source, target) in enumerate(((points, got_points), (slots, got))):
            pltpu.make_async_remote_copy(
                src_ref=source.at[owner],
                dst_ref=target.at[group, place],
                send_sem=sent.at[kind],
                recv_sem=got_sems.at[kind, group],
                device_id=there,
                device_id_type=MESH,
            ).start()

    total[...] = jnp.zeros_like(total)

    @pl.loop(0, src_count)
    def _(group):
        pltpu.make_async_copy(got_points.at[group], got_points.at[group], got_sems.at[0, group]).wait()
        pairs = got_points[group].reshape(tgt_count, lanes)
        col_x = [
            jnp.concatenate([pairs[i : i + 1, :capacity], pairs[i + 1 : i + 2, :capacity]], axis=1)
            for i in range(0, tgt_count, 2)
        ]
        col_y = [
            jnp.concatenate([pairs[i : i + 1, capacity:], pairs[i + 1 : i + 2, capacity:]], axis=1)
            for i in range(0, tgt_count, 2)
        ]
        for i in range(tgt_count // 2):
            cols[0:1, i * lanes : (i + 1) * lanes] = col_x[i]
            cols[1:2, i * lanes : (i + 1) * lanes] = col_y[i]
        pltpu.make_async_copy(got.at[group], got.at[group], got_sems.at[1, group]).wait()

        @pl.loop(0, rows // chunk)
        def _(part):
            @pl.loop(0, chunk // step)
            def _(index):
                here = pl.ds(pl.multiple_of(part * chunk + index * step, step), step)
                x, y = row_x[here, :], row_y[here, :]
                real_at = pl.ds(pl.multiple_of(index * step, step), step)
                imag_at = pl.ds(pl.multiple_of(chunk + index * step, step), step)
                for first in range(0, columns, lanes):
                    at = slice(first, first + lanes)
                    real, imag = kernel_values(x, y, cols[0:1, at], cols[1:2, at])
                    parts[real_at, at] = real
                    parts[imag_at, at] = imag

            weights = got[group].reshape(columns, width)
            both = jnp.dot(parts[...], weights, preferred_element_type=jnp.float32)
            crossed = both[chunk:]
            half = width // 2
            here = pl.ds(pl.multiple_of(part * chunk, chunk), chunk)
            total[here, :] += both[:chunk] + jnp.concatenate(
                [-crossed[:, half:], crossed[:, :half]], axis=1
            )

    out[...] = (total[...] * scale[...]).astype(jnp.bfloat16)
    rest = pl.ds(0, src_count * tgt_count - 1)
    for kind, source in enumerate((points, slots)):
        pltpu.make_async_copy(source.at[rest], source.at[rest], sent.at[kind]).wait()


def sketch_rows(row_first, impedance_rows, slots, points, mesh_shape, node_count):
    rows = impedance_rows.shape[0]
    count, capacity, width = slots.shape
    turn = node_count / 16.0 / (2.0 * math.pi)
    row_x, row_y = node_points(row_first + jnp.arange(rows, dtype=jnp.int32), node_count)
    spread = lambda v: jnp.broadcast_to(v[:, None], (rows, 128))
    columns = mesh_shape[1] * capacity
    vmem = pl.BlockSpec(memory_space=pltpu.VMEM)
    return pl.pallas_call(
        functools.partial(sketch_kernel, mesh_shape),
        out_shape=jax.ShapeDtypeStruct((rows, width), jnp.bfloat16),
        in_specs=[vmem] * 5,
        out_specs=vmem,
        scratch_shapes=[
            pltpu.VMEM((*mesh_shape, capacity, width), jnp.bfloat16),
            pltpu.VMEM((*mesh_shape, 1, 2 * capacity), jnp.float32),
            pltpu.VMEM((8, columns), jnp.float32),
            pltpu.VMEM((1024, columns), jnp.bfloat16),
            pltpu.VMEM((rows, width), jnp.float32),
            pltpu.SemaphoreType.DMA((2,)),
            pltpu.SemaphoreType.DMA((2, mesh_shape[0])),
        ],
        compiler_params=pltpu.CompilerParams(
            collective_id=1, has_side_effects=True, vmem_limit_bytes=48 << 20
        ),
    )(
        slots,
        points,
        spread(row_x * turn),
        spread(row_y * turn),
        spread(impedance_rows / math.sqrt(2.0 * math.pi)),
    )


def split(values, axis, order):
    high = values.astype(jnp.bfloat16)
    rest = values - high.astype(jnp.float32)
    middle = rest.astype(jnp.bfloat16)
    low = (rest - middle.astype(jnp.float32)).astype(jnp.bfloat16)
    pieces = (high, middle, low)
    return jnp.concatenate([pieces[i] for i in order], axis=axis)


LEFT, RIGHT = (0, 0, 1, 0, 1, 2), (0, 1, 0, 2, 1, 0)


def product(first, second, first_axis=1, second_axis=0):
    return lax.dot_general(
        split(first, first_axis, LEFT),
        split(second, second_axis, RIGHT),
        (((first_axis,), (second_axis,)), ((), ())),
        preferred_element_type=jnp.float32,
    )


def spread_rows(row, count):
    return jnp.broadcast_to(row, (count, row.shape[1]))


def eliminate_panel(panel, first, lanes):
    pieces = panel.shape[0] // 8
    rows = [panel[8 * i : 8 * i + 8] for i in range(pieces)]
    sublane = lax.broadcasted_iota(jnp.int32, (8, lanes), 0)
    twice = lambda v: jnp.concatenate([v, v], axis=1)
    done = []
    for top in range(pieces):
        columns = [
            [
                jnp.take_along_axis(
                    rows[i][:, :lanes],
                    jnp.full((8, lanes), first + 8 * top + t, jnp.int32),
                    axis=1,
                )
                for i in range(top, pieces)
            ]
            for t in range(8)
        ]
        for t in range(8):
            pivot = spread_rows(columns[t][0][t : t + 1], 8)
            inverse = 1.0 / pivot
            row = rows[top][t : t + 1]
            done.append(row * twice(lax.rsqrt(pivot[0:1])))
            factors = [c * inverse for c in columns[t]]
            factors[0] = jnp.where(sublane > t, factors[0], 0.0)
            for u in range(t + 1, 8):
                entry = spread_rows(columns[u][0][t : t + 1], 8)
                columns[u] = [c - f * entry for c, f in zip(columns[u], factors)]
            full_row = spread_rows(row, 8)
            for i, f in enumerate(factors):
                rows[top + i] = rows[top + i] - twice(f) * full_row
    return jnp.concatenate(done, axis=0)


def factor_solve(gram_matrix, right):
    size, block = gram_matrix.shape[0], 32
    diagonal = lax.broadcasted_iota(jnp.int32, (size, size), 0) == lax.broadcasted_iota(
        jnp.int32, (size, size), 1
    )
    trace = jnp.sum(jnp.where(diagonal, gram_matrix, 0.0), axis=(0, 1), keepdims=True)
    shifted = gram_matrix + jnp.where(diagonal, 0.25 * trace / size + 1e-06, 0.0)
    rest = jnp.concatenate([shifted, right], axis=1)
    solved = []
    for first in range(0, size, block):
        panel = eliminate_panel(rest[:block], first, size)
        solved.append(panel[:, size:])
        if first + block < size:
            rest = rest[block:] - product(panel[:, :size], panel, 0, 0)[first + block :]
    return jnp.concatenate(solved, axis=0)


def merge_kernel(rows, sketch, maps, out, sends, gots, send_sems, got_sems):
    src, tgt = lax.axis_index("src"), lax.axis_index("tgt")
    mates = (
        tgt + 1 - 2 * (tgt % 2),
        tgt + 2 - 4 * ((tgt // 2) % 2),
        tgt + 3 - 2 * (tgt % 4),
        tgt + 4 - 8 * ((tgt // 4) % 2),
    )
    barrier = pltpu.get_barrier_semaphore()
    for mate in mates:
        pl.semaphore_signal(barrier, inc=1, device_id=(src, mate), device_id_type=MESH)
    pl.semaphore_wait(barrier, len(mates))

    copies = []

    def post(values, targets):
        source = sends.at[sum(len(c) > 0 for c in copies)]
        source[...] = values
        base = sum(len(c) for c in copies)
        batch = []
        for i, target in enumerate(targets):
            copy = pltpu.make_async_remote_copy(
                src_ref=source,
                dst_ref=gots.at[base + i],
                send_sem=send_sems.at[base + i],
                recv_sem=got_sems.at[base + i],
                device_id=(src, mates[target]),
                device_id_type=MESH,
            )
            copy.start()
            batch.append((copy, base + i))
        copies.append(batch)
        return batch

    def take(batch):
        values = []
        for copy, slot in batch:
            copy.wait_recv()
            values.append(gots[slot])
        return values

    cross = lax.dot_general(
        sketch[...], sketch[...], (((0,), (0,)), ((), ())), preferred_element_type=jnp.float32
    )
    wide_maps = [maps[k].astype(jnp.float32) for k in range(4)]
    images = [product(cross, m) for m in wide_maps]
    gram_matrix = product(wide_maps[0], images[0], 0, 0) / rows
    turned = factor_solve(gram_matrix, wide_maps[0].T)
    for level in range(3):
        part = product(turned, images[level + 1]) / (rows * 2**level)
        if level == 0:
            batch = post(part, (0,))
            own = part
        else:
            batch = post(part, (0, 1, 2))
            near, far, beyond = take(batch)
            own = part + near
            if level == 1:
                other = far + beyond
            else:
                own = own + (far + beyond)
                batch = post(own, (3,))
        mine = product(own, own, 0, 0)
        right = product(own, turned, 0, 0)
        if level != 1:
            (other,) = take(batch)
        gram_matrix = (mine + product(other, other, 0, 0)) / 2.0
        turned = factor_solve(gram_matrix, right)
    for batch in copies:
        for copy, _ in batch:
            copy.wait_send()
    turned = split(turned, 1, (0, 1, 2))
    sketch_here = sketch[...]
    out[...] = lax.dot_general(
        jnp.concatenate([sketch_here] * 3, axis=1),
        turned,
        (((1,), (1,)), ((), ())),
        preferred_element_type=jnp.float32,
    )


def merged_bases(sketch, maps_here):
    rows, width = sketch.shape
    tile = (width, width)
    return pl.pallas_call(
        functools.partial(merge_kernel, rows),
        out_shape=jax.ShapeDtypeStruct((rows, width), jnp.float32),
        in_specs=[pl.BlockSpec(memory_space=pltpu.VMEM)] * 2,
        out_specs=pl.BlockSpec(memory_space=pltpu.VMEM),
        scratch_shapes=[
            pltpu.VMEM((4, *tile), jnp.float32),
            pltpu.VMEM((8, *tile), jnp.float32),
            pltpu.SemaphoreType.DMA((8,)),
            pltpu.SemaphoreType.DMA((8,)),
        ],
        compiler_params=pltpu.CompilerParams(
            collective_id=0, has_side_effects=True, vmem_limit_bytes=40 << 20
        ),
    )(sketch, maps_here)


def per_device(omega, owners, columns, impedance, level_maps):
    mesh_shape = (lax.axis_size("src"), lax.axis_size("tgt"))
    count = mesh_shape[0] * mesh_shape[1]
    rows = impedance.shape[0]
    node_count = mesh_shape[1] * rows
    slots, points = packed_slots(omega, owners, columns, count, node_count)
    sketch = sketch_rows(
        lax.axis_index("tgt") * rows,
        impedance,
        slots.reshape(count, -1, slots.shape[1]),
        points.reshape(count, 1, -1),
        mesh_shape,
        node_count,
    )
    return merged_bases(sketch, level_maps[0])[None]


def solution(mesh):
    in_specs = (
        P(("src", "tgt"), None),
        P(("src", "tgt"), None),
        P(("src", "tgt")),
        P("tgt"),
        P("src", None, None, None),
    )
    out_specs = P("src", "tgt", None)
    return jax.shard_map(
        per_device, mesh=mesh, in_specs=in_specs, out_specs=out_specs, check_vma=False
    )
```

```python
import functools
import math

import jax
import jax.numpy as jnp
from jax import lax
from jax.experimental import pallas as pl
from jax.experimental.pallas import tpu as pltpu
from jax.sharding import PartitionSpec as P

MESH = pl.DeviceIdType.MESH
SINE = (4.4415356787207045, -7.2646801556685014, 3.252047353220934)
COSINE = (1.414204078817102, -6.977641981219209, 5.715237646584958, -1.728346667500456)


def node_points(node_index, node_count):
    angles = 2.0 * math.pi / node_count * (node_index.astype(jnp.float32) + 0.5)
    radius = 1.0 + 0.25 * jnp.cos(3.0 * angles)
    return (radius * jnp.cos(angles), radius * jnp.sin(angles))


def pack_kernel(
    capacity,
    node_count,
    owners,
    columns,
    omega,
    chunks_out,
    places,
    placed,
    table,
    wide,
    plain,
    sem,
):
    blocks, lanes = owners.shape
    count, stride, _ = chunks_out.shape
    owner_at = lax.broadcasted_iota(jnp.int32, (count, lanes), 0)
    before = (
        lax.broadcasted_iota(jnp.int32, (lanes, lanes), 0)
        < lax.broadcasted_iota(jnp.int32, (lanes, lanes), 1)
    ).astype(jnp.float32)
    counted = jnp.concatenate([before, jnp.ones_like(before)], axis=1).astype(jnp.bfloat16)
    rank_at = lax.broadcasted_iota(jnp.int32, (capacity, lanes), 0)
    wide[...] = jnp.zeros_like(wide)
    table[...] = jnp.zeros_like(table)
    plain[...] = omega[...].astype(jnp.float32)

    def one_block(index, running):
        here = pl.ds(index, 1)
        owner, column = owners[here, :], columns[here, :]
        named = owner_at == owner
        onehot = named.astype(jnp.float32).astype(jnp.bfloat16)
        counts = jnp.dot(onehot, counted, preferred_element_type=jnp.float32)
        earlier = counts[:, :lanes] + running
        rank = jnp.sum(jnp.where(named, earlier, 0.0), axis=0, keepdims=True).astype(jnp.int32)
        places[here, :] = owner * stride + rank
        ranked = rank_at == rank
        digits = [
            jnp.where(ranked, digit.astype(jnp.float32), 0.0).astype(jnp.bfloat16)
            for digit in (column // 256, column % 256)
        ]
        table[...] += lax.dot_general(
            onehot,
            jnp.concatenate(digits, axis=0),
            (((1,), (1,)), ((), ())),
            preferred_element_type=jnp.float32,
        )
        return running + counts[:, lanes:]

    lax.fori_loop(0, blocks, one_block, jnp.zeros((count, lanes), jnp.float32), unroll=8)
    copy = pltpu.make_async_copy(places, placed, sem)
    copy.start()
    digits = table[...]
    column = digits[:, :capacity] * 256.0 + digits[:, capacity:]
    turn = node_count / 16.0 / (2.0 * math.pi)
    point = jnp.concatenate([v * turn for v in node_points(column, node_count)], axis=1)
    pieces = thirds(point)
    copy.wait()

    @pl.loop(0, blocks)
    def _(block):
        for first in range(0, lanes, 8):
            rows = plain[pl.ds(pl.multiple_of(block * lanes + first, 8), 8), :]
            for i in range(8):
                wide[pl.ds(placed[block, first + i], 1), :] = rows[i : i + 1]

    chunks_out[...] = wide[...].reshape(chunks_out.shape).astype(jnp.bfloat16)
    padding = jnp.zeros((count, stride - capacity - 3, lanes), jnp.float32)
    chunks_out[:, capacity:, :] = jnp.concatenate(
        [piece.astype(jnp.float32)[:, None, :] for piece in pieces] + [padding], axis=1
    ).astype(jnp.bfloat16)


def packed_chunks(omega, owners, columns, count, node_count):
    samples, width = omega.shape
    lanes = 128
    blocks = samples // lanes
    capacity = 2 * samples // count
    stride = capacity + 16
    vmem = pl.BlockSpec(memory_space=pltpu.VMEM)
    return pl.pallas_call(
        functools.partial(pack_kernel, capacity, node_count),
        out_shape=jax.ShapeDtypeStruct((count, stride, width), jnp.bfloat16),
        in_specs=[vmem] * 3,
        out_specs=vmem,
        scratch_shapes=[
            pltpu.VMEM((blocks, lanes), jnp.int32),
            pltpu.SMEM((blocks, lanes), jnp.int32),
            pltpu.VMEM((count, 2 * capacity), jnp.float32),
            pltpu.VMEM((count * stride, width), jnp.float32),
            pltpu.VMEM((samples, width), jnp.float32),
            pltpu.SemaphoreType.DMA,
        ],
        compiler_params=pltpu.CompilerParams(vmem_limit_bytes=40 << 20),
    )(owners.reshape(blocks, lanes), columns.reshape(blocks, lanes), omega)


def thirds(values):
    high = values.astype(jnp.bfloat16)
    rest = values - high.astype(jnp.float32)
    middle = rest.astype(jnp.bfloat16)
    low = (rest - middle.astype(jnp.float32)).astype(jnp.bfloat16)
    return high, middle, low


def kernel_values(x, y, col_x, col_y):
    dx = x - col_x
    dy = y - col_y
    square = jnp.maximum(dx * dx + dy * dy, 1e-30)
    turns = square * lax.rsqrt(square)
    part = turns - jnp.round(turns)
    amplitude = lax.rsqrt(turns + 0.5 / math.pi)
    z = part * part
    sine = part * (SINE[0] + z * (SINE[1] + z * SINE[2]))
    cosine = COSINE[0] + z * (COSINE[1] + z * (COSINE[2] + z * COSINE[3]))
    scaled = amplitude * sine
    return (amplitude - scaled * sine).astype(jnp.bfloat16), (scaled * cosine).astype(jnp.bfloat16)


def sketch_kernel(shape, capacity, chunks, row_x, row_y, scale, out, got, total, sent, got_sems):
    src_count, tgt_count = shape
    src, tgt = lax.axis_index("src"), lax.axis_index("tgt")
    rows, lanes = row_x.shape
    width = chunks.shape[2]
    turns = min(8, tgt_count)
    step, each = rows // turns, tgt_count // turns
    columns = tgt_count * capacity
    wrapped = lambda index, size: jnp.where(index >= size, index - size, index)

    def send(group, place):
        there = (wrapped(src + group, src_count), wrapped(tgt + place, tgt_count))
        pltpu.make_async_remote_copy(
            src_ref=chunks.at[there[0] * tgt_count + there[1]],
            dst_ref=got.at[group, place],
            send_sem=sent,
            recv_sem=got_sems.at[group],
            device_id=there,
            device_id_type=MESH,
        ).start()

    def greet(group, place):
        there = (wrapped(src + group, src_count), wrapped(tgt + place, tgt_count))
        pl.semaphore_signal(barrier, inc=1, device_id=there, device_id_type=MESH)

    barrier = pltpu.get_barrier_semaphore()

    @pl.loop(1, tgt_count)
    def _(place):
        greet(0, place)

    @pl.loop(1, src_count)
    def _(group):
        @pl.loop(0, tgt_count)
        def _(place):
            greet(group, place)

    pltpu.make_async_copy(chunks.at[src * tgt_count + tgt], got.at[0, 0], got_sems.at[0]).start()
    total[...] = jnp.zeros_like(total)
    pl.semaphore_wait(barrier, src_count * tgt_count - 1)

    @pl.loop(1, tgt_count)
    def _(place):
        send(0, place)

    def one_group(group, more):
        pltpu.make_async_copy(got.at[group], got.at[group], got_sems.at[group]).wait()
        pieces = got[group, :, capacity:, :].astype(jnp.float32)
        points = (pieces[:, 2] + pieces[:, 1]) + pieces[:, 0]
        join = lambda i, at: jnp.concatenate(
            [points[i : i + 1, at : at + capacity], points[i + 1 : i + 2, at : at + capacity]], axis=1
        )
        col_x = [join(i, 0) for i in range(0, tgt_count, 2)]
        col_y = [join(i, capacity) for i in range(0, tgt_count, 2)]
        weights = got[group, :, :capacity, :].reshape(columns, width)

        @pl.loop(0, rows // step)
        def _(index):
            if more:
                for i in range(each):
                    send(group + 1, index * each + i)
            here = pl.ds(pl.multiple_of(index * step, step), step)
            x, y = row_x[here, :], row_y[here, :]
            values = [kernel_values(x, y, a, b) for a, b in zip(col_x, col_y)]
            parts = jnp.concatenate(
                [jnp.concatenate([v[k] for v in values], axis=1) for k in (0, 1)], axis=0
            )
            both = jnp.dot(parts, weights, preferred_element_type=jnp.float32)
            crossed = both[step:]
            half = width // 2
            total[here, :] += both[:step] + jnp.concatenate(
                [-crossed[:, half:], crossed[:, :half]], axis=1
            )

    @pl.loop(0, src_count - 1)
    def _(group):
        one_group(group, True)

    one_group(src_count - 1, False)
    out[...] = (total[...] * scale[...]).astype(jnp.bfloat16)
    rest = chunks.at[pl.ds(0, src_count * tgt_count - 1)]
    pltpu.make_async_copy(rest, rest, sent).wait()


def sketch_rows(row_first, impedance_rows, chunks, mesh_shape, node_count):
    rows = impedance_rows.shape[0]
    count, stride, width = chunks.shape
    turn = node_count / 16.0 / (2.0 * math.pi)
    row_x, row_y = node_points(row_first + jnp.arange(rows, dtype=jnp.int32), node_count)
    spread = lambda v: jnp.broadcast_to(v[:, None], (rows, 128))
    vmem = pl.BlockSpec(memory_space=pltpu.VMEM)
    return pl.pallas_call(
        functools.partial(sketch_kernel, mesh_shape, stride - 16),
        out_shape=jax.ShapeDtypeStruct((rows, width), jnp.bfloat16),
        in_specs=[vmem] * 4,
        out_specs=vmem,
        scratch_shapes=[
            pltpu.VMEM((*mesh_shape, stride, width), jnp.bfloat16),
            pltpu.VMEM((rows, width), jnp.float32),
            pltpu.SemaphoreType.DMA,
            pltpu.SemaphoreType.DMA((mesh_shape[0],)),
        ],
        compiler_params=pltpu.CompilerParams(
            collective_id=1, has_side_effects=True, vmem_limit_bytes=48 << 20
        ),
    )(
        chunks,
        spread(row_x * turn),
        spread(row_y * turn),
        spread(impedance_rows / math.sqrt(2.0 * math.pi)),
    )


def split(values, axis, order):
    high = values.astype(jnp.bfloat16)
    rest = values - high.astype(jnp.float32)
    middle = rest.astype(jnp.bfloat16)
    low = (rest - middle.astype(jnp.float32)).astype(jnp.bfloat16)
    pieces = (high, middle, low)
    return jnp.concatenate([pieces[i] for i in order], axis=axis)


LEFT, RIGHT = (0, 0, 1, 0, 1, 2), (0, 1, 0, 2, 1, 0)


def product(first, second, first_axis=1, second_axis=0):
    return lax.dot_general(
        split(first, first_axis, LEFT),
        split(second, second_axis, RIGHT),
        (((first_axis,), (second_axis,)), ((), ())),
        preferred_element_type=jnp.float32,
    )


def spread_rows(row, count):
    return jnp.broadcast_to(row, (count, row.shape[1]))


def eliminate_panel(panel, first, lanes):
    pieces = panel.shape[0] // 8
    rows = [panel[8 * i : 8 * i + 8] for i in range(pieces)]
    sublane = lax.broadcasted_iota(jnp.int32, (8, lanes), 0)
    twice = lambda v: jnp.concatenate([v, v], axis=1)
    done = []
    for top in range(pieces):
        columns = [
            [
                jnp.take_along_axis(
                    rows[i][:, :lanes],
                    jnp.full((8, lanes), first + 8 * top + t, jnp.int32),
                    axis=1,
                )
                for i in range(top, pieces)
            ]
            for t in range(8)
        ]
        for t in range(8):
            pivot = spread_rows(columns[t][0][t : t + 1], 8)
            inverse = 1.0 / pivot
            row = rows[top][t : t + 1]
            done.append(row * twice(lax.rsqrt(pivot[0:1])))
            factors = [c * inverse for c in columns[t]]
            factors[0] = jnp.where(sublane > t, factors[0], 0.0)
            for u in range(t + 1, 8):
                entry = spread_rows(columns[u][0][t : t + 1], 8)
                columns[u] = [c - f * entry for c, f in zip(columns[u], factors)]
            full_row = spread_rows(row, 8)
            for i, f in enumerate(factors):
                rows[top + i] = rows[top + i] - twice(f) * full_row
    return jnp.concatenate(done, axis=0)


def factor_solve(gram_matrix, right):
    size, block = gram_matrix.shape[0], 32
    diagonal = lax.broadcasted_iota(jnp.int32, (size, size), 0) == lax.broadcasted_iota(
        jnp.int32, (size, size), 1
    )
    trace = jnp.sum(jnp.where(diagonal, gram_matrix, 0.0), axis=(0, 1), keepdims=True)
    shifted = gram_matrix + jnp.where(diagonal, 0.25 * trace / size + 1e-06, 0.0)
    rest = jnp.concatenate([shifted, right], axis=1)
    solved = []
    for first in range(0, size, block):
        panel = eliminate_panel(rest[:block], first, size)
        solved.append(panel[:, size:])
        if first + block < size:
            rest = rest[block:] - product(panel[:, :size], panel, 0, 0)[first + block :]
    return jnp.concatenate(solved, axis=0)


def merge_kernel(rows, sketch, maps, out, sends, gots, send_sems, got_sems):
    src, tgt = lax.axis_index("src"), lax.axis_index("tgt")
    mates = (
        tgt + 1 - 2 * (tgt % 2),
        tgt + 2 - 4 * ((tgt // 2) % 2),
        tgt + 3 - 2 * (tgt % 4),
        tgt + 4 - 8 * ((tgt // 4) % 2),
    )
    barrier = pltpu.get_barrier_semaphore()
    for mate in mates:
        pl.semaphore_signal(barrier, inc=1, device_id=(src, mate), device_id_type=MESH)
    pl.semaphore_wait(barrier, len(mates))

    copies = []

    def post(values, targets):
        source = sends.at[sum(len(c) > 0 for c in copies)]
        source[...] = values
        base = sum(len(c) for c in copies)
        batch = []
        for i, target in enumerate(targets):
            copy = pltpu.make_async_remote_copy(
                src_ref=source,
                dst_ref=gots.at[base + i],
                send_sem=send_sems.at[base + i],
                recv_sem=got_sems.at[base + i],
                device_id=(src, mates[target]),
                device_id_type=MESH,
            )
            copy.start()
            batch.append((copy, base + i))
        copies.append(batch)
        return batch

    def take(batch):
        values = []
        for copy, slot in batch:
            copy.wait_recv()
            values.append(gots[slot])
        return values

    cross = lax.dot_general(
        sketch[...], sketch[...], (((0,), (0,)), ((), ())), preferred_element_type=jnp.float32
    )
    wide_maps = [maps[k].astype(jnp.float32) for k in range(4)]
    images = [product(cross, m) for m in wide_maps]
    gram_matrix = product(wide_maps[0], images[0], 0, 0) / rows
    turned = factor_solve(gram_matrix, wide_maps[0].T)
    for level in range(3):
        part = product(turned, images[level + 1]) / (rows * 2**level)
        if level == 0:
            batch = post(part, (0,))
            own = part
        else:
            batch = post(part, (0, 1, 2))
            near, far, beyond = take(batch)
            own = part + near
            if level == 1:
                other = far + beyond
            else:
                own = own + (far + beyond)
                batch = post(own, (3,))
        mine = product(own, own, 0, 0)
        right = product(own, turned, 0, 0)
        if level != 1:
            (other,) = take(batch)
        gram_matrix = (mine + product(other, other, 0, 0)) / 2.0
        turned = factor_solve(gram_matrix, right)
    for batch in copies:
        for copy, _ in batch:
            copy.wait_send()
    turned = split(turned, 1, (0, 1, 2))
    sketch_here = sketch[...]
    out[...] = lax.dot_general(
        jnp.concatenate([sketch_here] * 3, axis=1),
        turned,
        (((1,), (1,)), ((), ())),
        preferred_element_type=jnp.float32,
    )


def merged_bases(sketch, maps_here):
    rows, width = sketch.shape
    tile = (width, width)
    return pl.pallas_call(
        functools.partial(merge_kernel, rows),
        out_shape=jax.ShapeDtypeStruct((rows, width), jnp.float32),
        in_specs=[pl.BlockSpec(memory_space=pltpu.VMEM)] * 2,
        out_specs=pl.BlockSpec(memory_space=pltpu.VMEM),
        scratch_shapes=[
            pltpu.VMEM((4, *tile), jnp.float32),
            pltpu.VMEM((8, *tile), jnp.float32),
            pltpu.SemaphoreType.DMA((8,)),
            pltpu.SemaphoreType.DMA((8,)),
        ],
        compiler_params=pltpu.CompilerParams(
            collective_id=0, has_side_effects=True, vmem_limit_bytes=40 << 20
        ),
    )(sketch, maps_here)


def sketch_of(omega, owners, columns, impedance):
    mesh_shape = (lax.axis_size("src"), lax.axis_size("tgt"))
    rows = impedance.shape[0]
    node_count = mesh_shape[1] * rows
    chunks = packed_chunks(omega, owners, columns, mesh_shape[0] * mesh_shape[1], node_count)
    first = lax.axis_index("tgt") * rows
    return sketch_rows(first, impedance, chunks, mesh_shape, node_count)


def per_device(omega, owners, columns, impedance, level_maps):
    return merged_bases(sketch_of(omega, owners, columns, impedance), level_maps[0])[None]


def solution(mesh):
    in_specs = (
        P(("src", "tgt"), None),
        P(("src", "tgt"), None),
        P(("src", "tgt")),
        P("tgt"),
        P("src", None, None, None),
    )
    out_specs = P("src", "tgt", None)
    return jax.shard_map(
        per_device, mesh=mesh, in_specs=in_specs, out_specs=out_specs, check_vma=False
    )
```

```python
import functools
import math

import jax
import jax.numpy as jnp
from jax import lax
from jax.experimental import pallas as pl
from jax.experimental.pallas import tpu as pltpu
from jax.sharding import PartitionSpec as P

MESH = pl.DeviceIdType.MESH
SINE = (4.4415356787207045, -7.2646801556685014, 3.252047353220934)
COSINE = (1.414204078817102, -6.977641981219209, 5.715237646584958, -1.728346667500456)


def node_points(node_index, node_count):
    angles = 2.0 * math.pi / node_count * (node_index.astype(jnp.float32) + 0.5)
    radius = 1.0 + 0.25 * jnp.cos(3.0 * angles)
    return (radius * jnp.cos(angles), radius * jnp.sin(angles))


def pack_kernel(
    capacity,
    node_count,
    owners,
    columns,
    omega,
    chunks_out,
    points_out,
    places,
    placed,
    table,
    wide,
    plain,
    sem,
):
    blocks, lanes = owners.shape
    count = points_out.shape[0]
    owner_at = lax.broadcasted_iota(jnp.int32, (count, lanes), 0)
    before = (
        lax.broadcasted_iota(jnp.int32, (lanes, lanes), 0)
        < lax.broadcasted_iota(jnp.int32, (lanes, lanes), 1)
    ).astype(jnp.float32)
    counted = jnp.concatenate([before, jnp.ones_like(before)], axis=1).astype(jnp.bfloat16)
    rank_at = lax.broadcasted_iota(jnp.int32, (capacity, lanes), 0)
    wide[...] = jnp.zeros_like(wide)
    table[...] = jnp.zeros_like(table)
    plain[...] = omega[...].astype(jnp.float32)

    def one_block(index, running):
        here = pl.ds(index, 1)
        owner, column = owners[here, :], columns[here, :]
        named = owner_at == owner
        onehot = named.astype(jnp.float32).astype(jnp.bfloat16)
        counts = jnp.dot(onehot, counted, preferred_element_type=jnp.float32)
        earlier = counts[:, :lanes] + running
        rank = jnp.sum(jnp.where(named, earlier, 0.0), axis=0, keepdims=True).astype(jnp.int32)
        places[here, :] = owner * capacity + rank
        ranked = rank_at == rank
        digits = [
            jnp.where(ranked, digit.astype(jnp.float32), 0.0).astype(jnp.bfloat16)
            for digit in (column // 256, column % 256)
        ]
        table[...] += lax.dot_general(
            onehot,
            jnp.concatenate(digits, axis=0),
            (((1,), (1,)), ((), ())),
            preferred_element_type=jnp.float32,
        )
        return running + counts[:, lanes:]

    lax.fori_loop(0, blocks, one_block, jnp.zeros((count, lanes), jnp.float32), unroll=8)
    copy = pltpu.make_async_copy(places, placed, sem)
    copy.start()
    digits = table[...]
    column = digits[:, :capacity] * 256.0 + digits[:, capacity:]
    turn = node_count / 16.0 / (2.0 * math.pi)
    point_x, point_y = node_points(column, node_count)
    points_out[...] = jnp.concatenate(gridded((point_x * turn, point_y * turn), 0.5), axis=1)
    copy.wait()

    @pl.loop(0, blocks)
    def _(block):
        for first in range(0, lanes, 8):
            rows = plain[pl.ds(pl.multiple_of(block * lanes + first, 8), 8), :]
            for i in range(8):
                wide[pl.ds(placed[block, first + i], 1), :] = rows[i : i + 1]

    chunks_out[...] = wide[...].astype(jnp.bfloat16)


def packed_chunks(omega, owners, columns, count, node_count):
    samples, width = omega.shape
    lanes = 128
    blocks = samples // lanes
    capacity = 2 * samples // count
    vmem = pl.BlockSpec(memory_space=pltpu.VMEM)
    return pl.pallas_call(
        functools.partial(pack_kernel, capacity, node_count),
        out_shape=(
            jax.ShapeDtypeStruct((count * capacity, width), jnp.bfloat16),
            jax.ShapeDtypeStruct((count, 2 * capacity), jnp.float32),
        ),
        in_specs=[vmem] * 3,
        out_specs=(vmem, vmem),
        scratch_shapes=[
            pltpu.VMEM((blocks, lanes), jnp.int32),
            pltpu.SMEM((blocks, lanes), jnp.int32),
            pltpu.VMEM((count, 2 * capacity), jnp.float32),
            pltpu.VMEM((count * capacity, width), jnp.float32),
            pltpu.VMEM((samples, width), jnp.float32),
            pltpu.SemaphoreType.DMA,
        ],
        compiler_params=pltpu.CompilerParams(vmem_limit_bytes=40 << 20),
    )(owners.reshape(blocks, lanes), columns.reshape(blocks, lanes), omega)


def gridded(points, shift):
    x, y = points
    return (jnp.floor(x * 16384.0 + (0.5 - shift)) + shift) / 16384.0, y


def kernel_values(x, y, col_x, col_y):
    dx = x - col_x
    dy = y - col_y
    square = dx * dx + dy * dy
    turns = square * lax.rsqrt(square)
    part = turns - jnp.round(turns)
    amplitude = lax.rsqrt(turns + 0.5 / math.pi)
    z = part * part
    sine = part * (SINE[0] + z * (SINE[1] + z * SINE[2]))
    cosine = COSINE[0] + z * (COSINE[1] + z * (COSINE[2] + z * COSINE[3]))
    scaled = amplitude * sine
    return (amplitude - scaled * sine).astype(jnp.bfloat16), (scaled * cosine).astype(jnp.bfloat16)


def sketch_kernel(
    sides, lead, chunks, points, row_x, row_y, scale, out, got, got_points, total, sent, got_sems
):
    src, tgt = lax.axis_index("src"), lax.axis_index("tgt")
    rows, lanes = row_x.shape
    count, capacity, width = chunks.shape
    groups, places = got.shape[:2]
    side_x, side_y, side_z = sides
    columns = places * capacity
    step, each = rows // 2, places // 2
    me = (src // 2, src % 2, tgt // side_z, tgt % side_z)

    def wrapped(index, size):
        return jnp.where(index >= size, index - size, index)

    def there(group, place):
        dx, dy, dz = place // side_y, place % side_y, group // 2
        for back in (dx, dy):
            dz = jnp.where(dz < back, dz + side_z - back, dz - back)
        core = wrapped(me[1] + group % 2, 2)
        return (
            2 * wrapped(me[0] + dx, side_x) + core,
            side_z * wrapped(me[2] + dy, side_y) + wrapped(me[3] + dz, side_z),
        )

    def each_other(first, last, act):
        for group in range(first, last):
            @pl.loop(1 if group == 0 else 0, places)
            def _(place):
                act(group, place)

    def greet(group, place):
        pl.semaphore_signal(barrier, inc=1, device_id=there(group, place), device_id_type=MESH)

    def send(group, place):
        target = there(group, place)
        owner = target[0] * side_y * side_z + target[1]
        for kind, (source, landing) in enumerate(((points, got_points), (chunks, got))):
            pltpu.make_async_remote_copy(
                src_ref=source.at[owner],
                dst_ref=landing.at[group, place],
                send_sem=sent.at[kind],
                recv_sem=got_sems.at[kind, group],
                device_id=target,
                device_id_type=MESH,
            ).start()

    barrier = pltpu.get_barrier_semaphore()
    each_other(0, groups, greet)
    own = src * side_y * side_z + tgt
    pltpu.make_async_copy(points.at[own], got_points.at[0, 0], got_sems.at[0, 0]).start()
    pltpu.make_async_copy(chunks.at[own], got.at[0, 0], got_sems.at[1, 0]).start()
    total[...] = jnp.zeros_like(total)
    pl.semaphore_wait(barrier, count - 1)
    each_other(0, lead, send)

    def one_group(group, more):
        for kind, landing in enumerate((got_points, got)):
            pltpu.make_async_copy(
                landing.at[group], landing.at[group], got_sems.at[kind, group]
            ).wait()
        pairs = got_points[group].reshape(places, 2 * capacity)
        join = lambda i, at: jnp.concatenate(
            [pairs[i : i + 1, at : at + capacity], pairs[i + 1 : i + 2, at : at + capacity]], axis=1
        )
        col_x = [join(i, 0) for i in range(0, places, 2)]
        col_y = [join(i, capacity) for i in range(0, places, 2)]
        weights = got[group].reshape(columns, width)

        @pl.loop(0, rows // step)
        def _(index):
            if more:
                for i in range(each):
                    send(group + lead, index * each + i)
            here = pl.ds(pl.multiple_of(index * step, step), step)
            x, y = row_x[here, :], row_y[here, :]
            values = [kernel_values(x, y, a, b) for a, b in zip(col_x, col_y)]
            parts = jnp.concatenate(
                [jnp.concatenate([v[k] for v in values], axis=1) for k in (0, 1)], axis=0
            )
            both = jnp.dot(parts, weights, preferred_element_type=jnp.float32)
            crossed = both[step:]
            half = width // 2
            total[here, :] += both[:step] + jnp.concatenate(
                [-crossed[:, half:], crossed[:, :half]], axis=1
            )

    @pl.loop(0, groups - lead)
    def _(group):
        one_group(group, True)

    @pl.loop(groups - lead, groups)
    def _(group):
        one_group(group, False)

    out[...] = (total[...] * scale[...]).astype(jnp.bfloat16)
    for kind, source in enumerate((points, chunks)):
        rest = source.at[pl.ds(0, count - 1)]
        pltpu.make_async_copy(rest, rest, sent.at[kind]).wait()


def sketch_rows(row_first, impedance_rows, chunks, points, mesh_shape, node_count):
    rows = impedance_rows.shape[0]
    count, capacity, width = chunks.shape
    side = math.isqrt(mesh_shape[1])
    sides = (mesh_shape[0] // 2, side, side)
    landing = (2 * side, count // (2 * side))
    turn = node_count / 16.0 / (2.0 * math.pi)
    row_x, row_y = node_points(row_first + jnp.arange(rows, dtype=jnp.int32), node_count)
    spread = lambda v: jnp.broadcast_to(v[:, None], (rows, 128))
    vmem = pl.BlockSpec(memory_space=pltpu.VMEM)
    return pl.pallas_call(
        functools.partial(sketch_kernel, sides, 3),
        out_shape=jax.ShapeDtypeStruct((rows, width), jnp.bfloat16),
        in_specs=[vmem] * 5,
        out_specs=vmem,
        scratch_shapes=[
            pltpu.VMEM((*landing, capacity, width), jnp.bfloat16),
            pltpu.VMEM((*landing, 1, 2 * capacity), jnp.float32),
            pltpu.VMEM((rows, width), jnp.float32),
            pltpu.SemaphoreType.DMA((2,)),
            pltpu.SemaphoreType.DMA((2, landing[0])),
        ],
        compiler_params=pltpu.CompilerParams(
            collective_id=1, has_side_effects=True, vmem_limit_bytes=48 << 20
        ),
    )(
        chunks,
        points,
        *(spread(v) for v in gridded((row_x * turn, row_y * turn), 0.0)),
        spread(impedance_rows / math.sqrt(2.0 * math.pi)),
    )


def split(values, axis, order):
    high = values.astype(jnp.bfloat16)
    rest = values - high.astype(jnp.float32)
    middle = rest.astype(jnp.bfloat16)
    low = (rest - middle.astype(jnp.float32)).astype(jnp.bfloat16)
    pieces = (high, middle, low)
    return jnp.concatenate([pieces[i] for i in order], axis=axis)


LEFT, RIGHT = (0, 0, 1, 0, 1, 2), (0, 1, 0, 2, 1, 0)


def product(first, second, first_axis=1, second_axis=0):
    return lax.dot_general(
        split(first, first_axis, LEFT),
        split(second, second_axis, RIGHT),
        (((first_axis,), (second_axis,)), ((), ())),
        preferred_element_type=jnp.float32,
    )


def spread_rows(row, count):
    return jnp.broadcast_to(row, (count, row.shape[1]))


def eliminate_panel(panel, first, lanes):
    pieces = panel.shape[0] // 8
    rows = [panel[8 * i : 8 * i + 8] for i in range(pieces)]
    sublane = lax.broadcasted_iota(jnp.int32, (8, lanes), 0)
    twice = lambda v: jnp.concatenate([v, v], axis=1)
    done = []
    for top in range(pieces):
        columns = [
            [
                jnp.take_along_axis(
                    rows[i][:, :lanes],
                    jnp.full((8, lanes), first + 8 * top + t, jnp.int32),
                    axis=1,
                )
                for i in range(top, pieces)
            ]
            for t in range(8)
        ]
        for t in range(8):
            pivot = spread_rows(columns[t][0][t : t + 1], 8)
            inverse = 1.0 / pivot
            row = rows[top][t : t + 1]
            done.append(row * twice(lax.rsqrt(pivot[0:1])))
            factors = [c * inverse for c in columns[t]]
            factors[0] = jnp.where(sublane > t, factors[0], 0.0)
            for u in range(t + 1, 8):
                entry = spread_rows(columns[u][0][t : t + 1], 8)
                columns[u] = [c - f * entry for c, f in zip(columns[u], factors)]
            full_row = spread_rows(row, 8)
            for i, f in enumerate(factors):
                rows[top + i] = rows[top + i] - twice(f) * full_row
    return jnp.concatenate(done, axis=0)


def factor_solve(gram_matrix, right):
    size, block = gram_matrix.shape[0], 32
    diagonal = lax.broadcasted_iota(jnp.int32, (size, size), 0) == lax.broadcasted_iota(
        jnp.int32, (size, size), 1
    )
    trace = jnp.sum(jnp.where(diagonal, gram_matrix, 0.0), axis=(0, 1), keepdims=True)
    shifted = gram_matrix + jnp.where(diagonal, 0.25 * trace / size + 1e-06, 0.0)
    rest = jnp.concatenate([shifted, right], axis=1)
    solved = []
    for first in range(0, size, block):
        panel = eliminate_panel(rest[:block], first, size)
        solved.append(panel[:, size:])
        if first + block < size:
            rest = rest[block:] - product(panel[:, :size], panel, 0, 0)[first + block :]
    return jnp.concatenate(solved, axis=0)


def merge_kernel(rows, sketch, maps, out, sends, gots, send_sems, got_sems):
    src, tgt = lax.axis_index("src"), lax.axis_index("tgt")
    mates = (
        tgt + 1 - 2 * (tgt % 2),
        tgt + 2 - 4 * ((tgt // 2) % 2),
        tgt + 3 - 2 * (tgt % 4),
        tgt + 4 - 8 * ((tgt // 4) % 2),
    )
    barrier = pltpu.get_barrier_semaphore()
    for mate in mates:
        pl.semaphore_signal(barrier, inc=1, device_id=(src, mate), device_id_type=MESH)
    copies = []

    def post(values, targets):
        source = sends.at[sum(len(c) > 0 for c in copies)]
        source[...] = values
        base = sum(len(c) for c in copies)
        batch = []
        for i, target in enumerate(targets):
            copy = pltpu.make_async_remote_copy(
                src_ref=source,
                dst_ref=gots.at[base + i],
                send_sem=send_sems.at[base + i],
                recv_sem=got_sems.at[base + i],
                device_id=(src, mates[target]),
                device_id_type=MESH,
            )
            copy.start()
            batch.append((copy, base + i))
        copies.append(batch)
        return batch

    def take(batch):
        values = []
        for copy, slot in batch:
            copy.wait_recv()
            values.append(gots[slot])
        return values

    cross = lax.dot_general(
        sketch[...], sketch[...], (((0,), (0,)), ((), ())), preferred_element_type=jnp.float32
    )
    wide_maps = [maps[k].astype(jnp.float32) for k in range(4)]
    images = [product(cross, m) for m in wide_maps]
    gram_matrix = product(wide_maps[0], images[0], 0, 0) / rows
    turned = factor_solve(gram_matrix, wide_maps[0].T)
    pl.semaphore_wait(barrier, len(mates))
    for level in range(3):
        part = product(turned, images[level + 1]) / (rows * 2**level)
        if level == 0:
            batch = post(part, (0,))
            own = part
        else:
            batch = post(part, (0, 1, 2))
            near, far, beyond = take(batch)
            own = part + near
            if level == 1:
                other = far + beyond
            else:
                own = own + (far + beyond)
                batch = post(own, (3,))
        mine = product(own, own, 0, 0)
        right = product(own, turned, 0, 0)
        if level != 1:
            (other,) = take(batch)
        gram_matrix = (mine + product(other, other, 0, 0)) / 2.0
        turned = factor_solve(gram_matrix, right)
    for batch in copies:
        for copy, _ in batch:
            copy.wait_send()
    turned = split(turned, 1, (0, 1, 2))
    sketch_here = sketch[...]
    out[...] = lax.dot_general(
        jnp.concatenate([sketch_here] * 3, axis=1),
        turned,
        (((1,), (1,)), ((), ())),
        preferred_element_type=jnp.float32,
    )


def merged_bases(sketch, maps_here):
    rows, width = sketch.shape
    tile = (width, width)
    return pl.pallas_call(
        functools.partial(merge_kernel, rows),
        out_shape=jax.ShapeDtypeStruct((rows, width), jnp.float32),
        in_specs=[pl.BlockSpec(memory_space=pltpu.VMEM)] * 2,
        out_specs=pl.BlockSpec(memory_space=pltpu.VMEM),
        scratch_shapes=[
            pltpu.VMEM((4, *tile), jnp.float32),
            pltpu.VMEM((8, *tile), jnp.float32),
            pltpu.SemaphoreType.DMA((8,)),
            pltpu.SemaphoreType.DMA((8,)),
        ],
        compiler_params=pltpu.CompilerParams(
            collective_id=0, has_side_effects=True, vmem_limit_bytes=40 << 20
        ),
    )(sketch, maps_here)


def sketch_of(omega, owners, columns, impedance):
    mesh_shape = (lax.axis_size("src"), lax.axis_size("tgt"))
    rows = impedance.shape[0]
    node_count = mesh_shape[1] * rows
    count = mesh_shape[0] * mesh_shape[1]
    chunks, points = packed_chunks(omega, owners, columns, count, node_count)
    chunks = chunks.reshape(count, -1, chunks.shape[1])
    points = points.reshape(count, 1, -1)
    first = lax.axis_index("tgt") * rows
    return sketch_rows(first, impedance, chunks, points, mesh_shape, node_count)


def per_device(omega, owners, columns, impedance, level_maps):
    return merged_bases(sketch_of(omega, owners, columns, impedance), level_maps[0])[None]


def solution(mesh):
    in_specs = (
        P(("src", "tgt"), None),
        P(("src", "tgt"), None),
        P(("src", "tgt")),
        P("tgt"),
        P("src", None, None, None),
    )
    out_specs = P("src", "tgt", None)
    return jax.shard_map(
        per_device, mesh=mesh, in_specs=in_specs, out_specs=out_specs, check_vma=False
    )
```

```python
import functools
import math

import jax
import jax.numpy as jnp
from jax import lax
from jax.experimental import pallas as pl
from jax.experimental.pallas import tpu as pltpu
from jax.sharding import PartitionSpec as P

MESH = pl.DeviceIdType.MESH
SINE = (4.4415356787207045, -7.2646801556685014, 3.252047353220934)
COSINE = (1.414204078817102, -6.977641981219209, 5.715237646584958, -1.728346667500456)


def node_points(node_index, node_count):
    angles = 2.0 * math.pi / node_count * (node_index.astype(jnp.float32) + 0.5)
    radius = 1.0 + 0.25 * jnp.cos(3.0 * angles)
    return (radius * jnp.cos(angles), radius * jnp.sin(angles))


def pack_kernel(
    capacity,
    node_count,
    owners,
    columns,
    omega,
    chunks_out,
    points_out,
    places,
    placed,
    table,
    wide,
    plain,
    sem,
):
    blocks, lanes = owners.shape
    count = points_out.shape[0]
    owner_at = lax.broadcasted_iota(jnp.int32, (count, lanes), 0)
    before = (
        lax.broadcasted_iota(jnp.int32, (lanes, lanes), 0)
        < lax.broadcasted_iota(jnp.int32, (lanes, lanes), 1)
    ).astype(jnp.float32)
    counted = jnp.concatenate([before, jnp.ones_like(before)], axis=1).astype(jnp.bfloat16)
    rank_at = lax.broadcasted_iota(jnp.int32, (capacity, lanes), 0)
    wide[...] = jnp.zeros_like(wide)
    table[...] = jnp.zeros_like(table)
    plain[...] = omega[...].astype(jnp.float32)

    def one_block(index, running):
        here = pl.ds(index, 1)
        owner, column = owners[here, :], columns[here, :]
        named = owner_at == owner
        onehot = named.astype(jnp.float32).astype(jnp.bfloat16)
        counts = jnp.dot(onehot, counted, preferred_element_type=jnp.float32)
        earlier = counts[:, :lanes] + running
        rank = jnp.sum(jnp.where(named, earlier, 0.0), axis=0, keepdims=True).astype(jnp.int32)
        places[here, :] = owner * capacity + rank
        ranked = rank_at == rank
        digits = [
            jnp.where(ranked, digit.astype(jnp.float32), 0.0).astype(jnp.bfloat16)
            for digit in (column // 256, column % 256)
        ]
        table[...] += lax.dot_general(
            onehot,
            jnp.concatenate(digits, axis=0),
            (((1,), (1,)), ((), ())),
            preferred_element_type=jnp.float32,
        )
        return running + counts[:, lanes:]

    lax.fori_loop(0, blocks, one_block, jnp.zeros((count, lanes), jnp.float32), unroll=8)
    copy = pltpu.make_async_copy(places, placed, sem)
    copy.start()
    digits = table[...]
    column = digits[:, :capacity] * 256.0 + digits[:, capacity:]
    turn = node_count / 16.0 / (2.0 * math.pi)
    point_x, point_y = node_points(column, node_count)
    points_out[...] = jnp.concatenate(gridded((point_x * turn, point_y * turn), 0.5), axis=1)
    copy.wait()

    @pl.loop(0, blocks)
    def _(block):
        for first in range(0, lanes, 8):
            rows = plain[pl.ds(pl.multiple_of(block * lanes + first, 8), 8), :]
            for i in range(8):
                wide[pl.ds(placed[block, first + i], 1), :] = rows[i : i + 1]

    chunks_out[...] = wide[...].astype(jnp.bfloat16)


def packed_chunks(omega, owners, columns, count, node_count):
    samples, width = omega.shape
    lanes = 128
    blocks = samples // lanes
    capacity = 2 * samples // count
    vmem = pl.BlockSpec(memory_space=pltpu.VMEM)
    return pl.pallas_call(
        functools.partial(pack_kernel, capacity, node_count),
        out_shape=(
            jax.ShapeDtypeStruct((count * capacity, width), jnp.bfloat16),
            jax.ShapeDtypeStruct((count, 2 * capacity), jnp.float32),
        ),
        in_specs=[vmem] * 3,
        out_specs=(vmem, vmem),
        scratch_shapes=[
            pltpu.VMEM((blocks, lanes), jnp.int32),
            pltpu.SMEM((blocks, lanes), jnp.int32),
            pltpu.VMEM((count, 2 * capacity), jnp.float32),
            pltpu.VMEM((count * capacity, width), jnp.float32),
            pltpu.VMEM((samples, width), jnp.float32),
            pltpu.SemaphoreType.DMA,
        ],
        compiler_params=pltpu.CompilerParams(vmem_limit_bytes=40 << 20),
    )(owners.reshape(blocks, lanes), columns.reshape(blocks, lanes), omega)


def gridded(points, shift):
    x, y = points
    return (jnp.floor(x * 16384.0 + (0.5 - shift)) + shift) / 16384.0, y


def kernel_values(x, y, col_x, col_y):
    dx = x - col_x
    dy = y - col_y
    square = dx * dx + dy * dy
    turns = square * lax.rsqrt(square)
    part = turns - jnp.round(turns)
    amplitude = lax.rsqrt(turns + 0.5 / math.pi)
    z = part * part
    sine = part * (SINE[0] + z * (SINE[1] + z * SINE[2]))
    cosine = COSINE[0] / COSINE[3] + z * (COSINE[1] / COSINE[3] + z * (COSINE[2] / COSINE[3] + z))
    scaled = amplitude * sine
    return (amplitude - scaled * sine).astype(jnp.bfloat16), (scaled * cosine).astype(jnp.bfloat16)


def sketch_kernel(
    sides,
    lead,
    chunks,
    points,
    row_table,
    out,
    got,
    got_points,
    row_values,
    total,
    sent,
    got_sems,
):
    src, tgt = lax.axis_index("src"), lax.axis_index("tgt")
    rows, lanes = total.shape[1:]
    count, capacity, width = chunks.shape
    groups, places = got.shape[:2]
    side_x, side_y, side_z = sides
    columns = places * capacity
    blocks = rows // lanes
    me = (src // 2, src % 2, tgt // side_z, tgt % side_z)

    def wrapped(index, size):
        return jnp.where(index >= size, index - size, index)

    def there(group, place):
        dx, dy, dz = place // side_y, place % side_y, group // 2
        for back in (dx, dy):
            dz = jnp.where(dz < back, dz + side_z - back, dz - back)
        core = wrapped(me[1] + group % 2, 2)
        return (
            2 * wrapped(me[0] + dx, side_x) + core,
            side_z * wrapped(me[2] + dy, side_y) + wrapped(me[3] + dz, side_z),
        )

    def each_other(first, last, act):
        for group in range(first, last):
            @pl.loop(1 if group == 0 else 0, places)
            def _(place):
                act(group, place)

    def greet(group, place):
        pl.semaphore_signal(barrier, inc=1, device_id=there(group, place), device_id_type=MESH)

    def send(group, place):
        target = there(group, place)
        owner = target[0] * side_y * side_z + target[1]
        for kind, (source, landing) in enumerate(((points, got_points), (chunks, got))):
            pltpu.make_async_remote_copy(
                src_ref=source.at[owner],
                dst_ref=landing.at[group, place],
                send_sem=sent.at[kind],
                recv_sem=got_sems.at[kind, group],
                device_id=target,
                device_id_type=MESH,
            ).start()

    barrier = pltpu.get_barrier_semaphore()
    each_other(0, groups, greet)
    own = src * side_y * side_z + tgt
    pltpu.make_async_copy(points.at[own], got_points.at[0, 0], got_sems.at[0, 0]).start()
    pltpu.make_async_copy(chunks.at[own], got.at[0, 0], got_sems.at[1, 0]).start()
    total[...] = jnp.zeros_like(total)
    pl.semaphore_wait(barrier, count - 1)
    each_other(0, lead, send)
    turned = row_table[...].T
    for kind in range(3):
        for block in range(blocks):
            at = jnp.full((lanes, lanes), kind * blocks + block, jnp.int32)
            row_values[kind, block * lanes : (block + 1) * lanes, :] = jnp.take_along_axis(
                turned, at, axis=1
            )

    def one_group(group, more):
        for kind, landing in enumerate((got_points, got)):
            pltpu.make_async_copy(
                landing.at[group], landing.at[group], got_sems.at[kind, group]
            ).wait()
        pairs = got_points[group].reshape(places, 2 * capacity)
        join = lambda i, at: jnp.concatenate(
            [pairs[i : i + 1, at : at + capacity], pairs[i + 1 : i + 2, at : at + capacity]], axis=1
        )
        col_x = [join(i, 0) for i in range(0, places, 2)]
        col_y = [join(i, capacity) for i in range(0, places, 2)]
        weights = got[group].reshape(columns, width)

        if more:
            @pl.loop(0, places)
            def _(place):
                send(group + lead, place)
        x, y = row_values[0], row_values[1]
        values = [kernel_values(x, y, a, b) for a, b in zip(col_x, col_y)]
        parts = jnp.concatenate(
            [jnp.concatenate([v[k] for v in values], axis=1) for k in (0, 1)], axis=0
        )
        both = jnp.dot(parts, weights, preferred_element_type=jnp.float32)
        total[0] += both[:rows]
        total[1] += both[rows:]

    @pl.loop(0, groups - lead)
    def _(group):
        one_group(group, True)

    @pl.loop(groups - lead, groups)
    def _(group):
        one_group(group, False)

    half = width // 2
    crossed = total[1] * COSINE[3]
    product = total[0] + jnp.concatenate([-crossed[:, half:], crossed[:, :half]], axis=1)
    out[...] = (product * row_values[2]).astype(jnp.bfloat16)
    for kind, source in enumerate((points, chunks)):
        rest = source.at[pl.ds(0, count - 1)]
        pltpu.make_async_copy(rest, rest, sent.at[kind]).wait()


def sketch_rows(row_first, impedance_rows, chunks, points, mesh_shape, node_count):
    rows = impedance_rows.shape[0]
    count, capacity, width = chunks.shape
    side = math.isqrt(mesh_shape[1])
    sides = (mesh_shape[0] // 2, side, side)
    landing = (2 * side, count // (2 * side))
    turn = node_count / 16.0 / (2.0 * math.pi)
    row_x, row_y = node_points(row_first + jnp.arange(rows, dtype=jnp.int32), node_count)
    scale = impedance_rows / math.sqrt(2.0 * math.pi)
    row_values = (*gridded((row_x * turn, row_y * turn), 0.0), scale)
    table = jnp.concatenate([v.reshape(-1, 128) for v in row_values], axis=0)
    table = jnp.pad(table, ((0, 128 - table.shape[0]), (0, 0)))
    vmem = pl.BlockSpec(memory_space=pltpu.VMEM)
    return pl.pallas_call(
        functools.partial(sketch_kernel, sides, 3),
        out_shape=jax.ShapeDtypeStruct((rows, width), jnp.bfloat16),
        in_specs=[vmem] * 3,
        out_specs=vmem,
        scratch_shapes=[
            pltpu.VMEM((*landing, capacity, width), jnp.bfloat16),
            pltpu.VMEM((*landing, 1, 2 * capacity), jnp.float32),
            pltpu.VMEM((3, rows, 128), jnp.float32),
            pltpu.VMEM((2, rows, width), jnp.float32),
            pltpu.SemaphoreType.DMA((2,)),
            pltpu.SemaphoreType.DMA((2, landing[0])),
        ],
        compiler_params=pltpu.CompilerParams(
            collective_id=1, has_side_effects=True, vmem_limit_bytes=48 << 20
        ),
    )(
        chunks,
        points,
        table,
    )


def split(values, axis, order):
    high = values.astype(jnp.bfloat16)
    rest = values - high.astype(jnp.float32)
    middle = rest.astype(jnp.bfloat16)
    low = (rest - middle.astype(jnp.float32)).astype(jnp.bfloat16)
    pieces = (high, middle, low)
    return jnp.concatenate([pieces[i] for i in order], axis=axis)


LEFT, RIGHT = (0, 0, 1, 0, 1, 2), (0, 1, 0, 2, 1, 0)


def product(first, second, first_axis=1, second_axis=0):
    return lax.dot_general(
        split(first, first_axis, LEFT),
        split(second, second_axis, RIGHT),
        (((first_axis,), (second_axis,)), ((), ())),
        preferred_element_type=jnp.float32,
    )


def spread_rows(row, count):
    return jnp.broadcast_to(row, (count, row.shape[1]))


def eliminate_panel(panel, first, lanes):
    pieces = panel.shape[0] // 8
    rows = [panel[8 * i : 8 * i + 8] for i in range(pieces)]
    sublane = lax.broadcasted_iota(jnp.int32, (8, lanes), 0)
    twice = lambda v: jnp.concatenate([v, v], axis=1)
    done = []
    for top in range(0, pieces, 2):
        columns = [
            {
                i: jnp.take_along_axis(
                    rows[i][:, :lanes],
                    jnp.full((8, lanes), first + 8 * top + t, jnp.int32),
                    axis=1,
                )
                for i in range(top, pieces)
            }
            for t in range(16)
        ]
        for t in range(16):
            here, at = top + t // 8, t % 8
            pivot = spread_rows(columns[t][here][at : at + 1], 8)
            inverse = 1.0 / pivot
            row = rows[here][at : at + 1]
            done.append(row * twice(lax.rsqrt(pivot[0:1])))
            factors = {i: columns[t][i] * inverse for i in range(here, pieces)}
            factors[here] = jnp.where(sublane > at, factors[here], 0.0)
            for u in range(t + 1, 16):
                entry = spread_rows(columns[u][here][at : at + 1], 8)
                for i, f in factors.items():
                    columns[u][i] = columns[u][i] - f * entry
            full_row = spread_rows(row, 8)
            for i, f in factors.items():
                rows[i] = rows[i] - twice(f) * full_row
    return jnp.concatenate(done, axis=0)


def factor_solve(gram_matrix, right):
    size, block = gram_matrix.shape[0], 32
    diagonal = lax.broadcasted_iota(jnp.int32, (size, size), 0) == lax.broadcasted_iota(
        jnp.int32, (size, size), 1
    )
    trace = jnp.sum(jnp.where(diagonal, gram_matrix, 0.0), axis=(0, 1), keepdims=True)
    shifted = gram_matrix + jnp.where(diagonal, 0.25 * trace / size + 1e-06, 0.0)
    rest = jnp.concatenate([shifted, right], axis=1)
    solved = []
    for first in range(0, size, block):
        panel = eliminate_panel(rest[:block], first, size)
        solved.append(panel[:, size:])
        if first + block < size:
            rest = rest[block:] - product(panel[:, :size], panel, 0, 0)[first + block :]
    return jnp.concatenate(solved, axis=0)


def merge_kernel(rows, sketch, maps, out, sends, gots, send_sems, got_sems):
    src, tgt = lax.axis_index("src"), lax.axis_index("tgt")
    mates = (
        tgt + 1 - 2 * (tgt % 2),
        tgt + 2 - 4 * ((tgt // 2) % 2),
        tgt + 3 - 2 * (tgt % 4),
        tgt + 4 - 8 * ((tgt // 4) % 2),
    )
    barrier = pltpu.get_barrier_semaphore()
    for mate in mates:
        pl.semaphore_signal(barrier, inc=1, device_id=(src, mate), device_id_type=MESH)
    copies = []

    def post(values, targets):
        source = sends.at[sum(len(c) > 0 for c in copies)]
        source[...] = values
        base = sum(len(c) for c in copies)
        batch = []
        for i, target in enumerate(targets):
            copy = pltpu.make_async_remote_copy(
                src_ref=source,
                dst_ref=gots.at[base + i],
                send_sem=send_sems.at[base + i],
                recv_sem=got_sems.at[base + i],
                device_id=(src, mates[target]),
                device_id_type=MESH,
            )
            copy.start()
            batch.append((copy, base + i))
        copies.append(batch)
        return batch

    def take(batch):
        values = []
        for copy, slot in batch:
            copy.wait_recv()
            values.append(gots[slot])
        return values

    cross = lax.dot_general(
        sketch[...], sketch[...], (((0,), (0,)), ((), ())), preferred_element_type=jnp.float32
    )
    wide_maps = [maps[k].astype(jnp.float32) for k in range(4)]
    images = [product(cross, m) for m in wide_maps]
    gram_matrix = product(wide_maps[0], images[0], 0, 0) / rows
    turned = factor_solve(gram_matrix, wide_maps[0].T)
    pl.semaphore_wait(barrier, len(mates))
    for level in range(3):
        part = product(turned, images[level + 1]) / (rows * 2**level)
        if level == 0:
            batch = post(part, (0,))
            own = part
        else:
            batch = post(part, (0, 1, 2))
            near, far, beyond = take(batch)
            own = part + near
            if level == 1:
                other = far + beyond
            else:
                own = own + (far + beyond)
                batch = post(own, (3,))
        mine = product(own, own, 0, 0)
        right = product(own, turned, 0, 0)
        if level != 1:
            (other,) = take(batch)
        gram_matrix = (mine + product(other, other, 0, 0)) / 2.0
        turned = factor_solve(gram_matrix, right)
    for batch in copies:
        for copy, _ in batch:
            copy.wait_send()
    turned = split(turned, 1, (0, 1, 2))
    sketch_here = sketch[...]
    out[...] = lax.dot_general(
        jnp.concatenate([sketch_here] * 3, axis=1),
        turned,
        (((1,), (1,)), ((), ())),
        preferred_element_type=jnp.float32,
    )


def merged_bases(sketch, maps_here):
    rows, width = sketch.shape
    tile = (width, width)
    return pl.pallas_call(
        functools.partial(merge_kernel, rows),
        out_shape=jax.ShapeDtypeStruct((rows, width), jnp.float32),
        in_specs=[pl.BlockSpec(memory_space=pltpu.VMEM)] * 2,
        out_specs=pl.BlockSpec(memory_space=pltpu.VMEM),
        scratch_shapes=[
            pltpu.VMEM((4, *tile), jnp.float32),
            pltpu.VMEM((8, *tile), jnp.float32),
            pltpu.SemaphoreType.DMA((8,)),
            pltpu.SemaphoreType.DMA((8,)),
        ],
        compiler_params=pltpu.CompilerParams(
            collective_id=0, has_side_effects=True, vmem_limit_bytes=40 << 20
        ),
    )(sketch, maps_here)


def sketch_of(omega, owners, columns, impedance):
    mesh_shape = (lax.axis_size("src"), lax.axis_size("tgt"))
    rows = impedance.shape[0]
    node_count = mesh_shape[1] * rows
    count = mesh_shape[0] * mesh_shape[1]
    chunks, points = packed_chunks(omega, owners, columns, count, node_count)
    chunks = chunks.reshape(count, -1, chunks.shape[1])
    points = points.reshape(count, 1, -1)
    first = lax.axis_index("tgt") * rows
    return sketch_rows(first, impedance, chunks, points, mesh_shape, node_count)


def per_device(omega, owners, columns, impedance, level_maps):
    return merged_bases(sketch_of(omega, owners, columns, impedance), level_maps[0])[None]


def solution(mesh):
    in_specs = (
        P(("src", "tgt"), None),
        P(("src", "tgt"), None),
        P(("src", "tgt")),
        P("tgt"),
        P("src", None, None, None),
    )
    out_specs = P("src", "tgt", None)
    return jax.shard_map(
        per_device, mesh=mesh, in_specs=in_specs, out_specs=out_specs, check_vma=False
    )
```

```python
import functools
import math

import jax
import jax.numpy as jnp
from jax import lax
from jax.experimental import pallas as pl
from jax.experimental.pallas import tpu as pltpu
from jax.sharding import PartitionSpec as P

MESH = pl.DeviceIdType.MESH
SINE = (4.4415356787207045, -7.2646801556685014, 3.252047353220934)
COSINE = (1.414204078817102, -6.977641981219209, 5.715237646584958, -1.728346667500456)


def node_points(node_index, node_count):
    angles = 2.0 * math.pi / node_count * (node_index.astype(jnp.float32) + 0.5)
    radius = 1.0 + 0.25 * jnp.cos(3.0 * angles)
    return (radius * jnp.cos(angles), radius * jnp.sin(angles))


def pack_kernel(
    capacity,
    node_count,
    owners,
    columns,
    omega,
    chunks_out,
    points_out,
    places,
    placed,
    table,
    wide,
    plain,
    sem,
):
    blocks, lanes = owners.shape
    count = points_out.shape[0]
    owner_at = lax.broadcasted_iota(jnp.int32, (count, lanes), 0)
    before = (
        lax.broadcasted_iota(jnp.int32, (lanes, lanes), 0)
        < lax.broadcasted_iota(jnp.int32, (lanes, lanes), 1)
    ).astype(jnp.float32)
    counted = jnp.concatenate([before, jnp.ones_like(before)], axis=1).astype(jnp.bfloat16)
    rank_at = lax.broadcasted_iota(jnp.int32, (capacity, lanes), 0)
    wide[...] = jnp.zeros_like(wide)
    table[...] = jnp.zeros_like(table)
    plain[...] = omega[...].astype(jnp.float32)

    def one_block(index, running):
        here = pl.ds(index, 1)
        owner, column = owners[here, :], columns[here, :]
        named = owner_at == owner
        onehot = named.astype(jnp.float32).astype(jnp.bfloat16)
        counts = jnp.dot(onehot, counted, preferred_element_type=jnp.float32)
        earlier = counts[:, :lanes] + running
        rank = jnp.sum(jnp.where(named, earlier, 0.0), axis=0, keepdims=True).astype(jnp.int32)
        places[here, :] = owner * capacity + rank
        ranked = rank_at == rank
        digits = [
            jnp.where(ranked, digit.astype(jnp.float32), 0.0).astype(jnp.bfloat16)
            for digit in (column // 256, column % 256)
        ]
        table[...] += lax.dot_general(
            onehot,
            jnp.concatenate(digits, axis=0),
            (((1,), (1,)), ((), ())),
            preferred_element_type=jnp.float32,
        )
        return running + counts[:, lanes:]

    lax.fori_loop(0, blocks, one_block, jnp.zeros((count, lanes), jnp.float32), unroll=8)
    copy = pltpu.make_async_copy(places, placed, sem)
    copy.start()
    digits = table[...]
    column = digits[:, :capacity] * 256.0 + digits[:, capacity:]
    turn = node_count / 16.0 / (2.0 * math.pi)
    point_x, point_y = node_points(column, node_count)
    points_out[...] = jnp.concatenate(gridded((point_x * turn, point_y * turn), 0.5), axis=1)
    copy.wait()

    @pl.loop(0, blocks)
    def _(block):
        for first in range(0, lanes, 8):
            rows = plain[pl.ds(pl.multiple_of(block * lanes + first, 8), 8), :]
            for i in range(8):
                wide[pl.ds(placed[block, first + i], 1), :] = rows[i : i + 1]

    chunks_out[...] = wide[...].astype(jnp.bfloat16)


def packed_chunks(omega, owners, columns, count, node_count):
    samples, width = omega.shape
    lanes = 128
    blocks = samples // lanes
    capacity = 2 * samples // count
    vmem = pl.BlockSpec(memory_space=pltpu.VMEM)
    return pl.pallas_call(
        functools.partial(pack_kernel, capacity, node_count),
        out_shape=(
            jax.ShapeDtypeStruct((count * capacity, width), jnp.bfloat16),
            jax.ShapeDtypeStruct((count, 2 * capacity), jnp.float32),
        ),
        in_specs=[vmem] * 3,
        out_specs=(vmem, vmem),
        scratch_shapes=[
            pltpu.VMEM((blocks, lanes), jnp.int32),
            pltpu.SMEM((blocks, lanes), jnp.int32),
            pltpu.VMEM((count, 2 * capacity), jnp.float32),
            pltpu.VMEM((count * capacity, width), jnp.float32),
            pltpu.VMEM((samples, width), jnp.float32),
            pltpu.SemaphoreType.DMA,
        ],
        compiler_params=pltpu.CompilerParams(vmem_limit_bytes=40 << 20),
    )(owners.reshape(blocks, lanes), columns.reshape(blocks, lanes), omega)


def gridded(points, shift):
    x, y = points
    return (jnp.floor(x * 16384.0 + (0.5 - shift)) + shift) / 16384.0, y


def kernel_values(x, y, col_x, col_y):
    dx = x - col_x
    dy = y - col_y
    square = dx * dx + dy * dy
    turns = square * lax.rsqrt(square)
    part = turns - jnp.round(turns)
    amplitude = lax.rsqrt(turns + 0.5 / math.pi)
    z = part * part
    sine = part * (SINE[0] + z * (SINE[1] + z * SINE[2]))
    cosine = COSINE[0] / COSINE[3] + z * (COSINE[1] / COSINE[3] + z * (COSINE[2] / COSINE[3] + z))
    scaled = amplitude * sine
    return (amplitude - scaled * sine).astype(jnp.bfloat16), (scaled * cosine).astype(jnp.bfloat16)


def sketch_kernel(
    sides,
    lead,
    chunks,
    points,
    row_table,
    out,
    got,
    got_points,
    row_values,
    total,
    sent,
    got_sems,
):
    src, tgt = lax.axis_index("src"), lax.axis_index("tgt")
    rows, lanes = total.shape[1:]
    count, capacity, width = chunks.shape
    groups, places = got.shape[:2]
    side_x, side_y, side_z = sides
    columns = places * capacity
    blocks = rows // lanes
    me = (src // 2, src % 2, tgt // side_z, tgt % side_z)

    def wrapped(index, size):
        return jnp.where(index >= size, index - size, index)

    def there(group, place):
        dx, dy, dz = place // side_y, place % side_y, group // 2
        for back in (dx, dy):
            dz = jnp.where(dz < back, dz + side_z - back, dz - back)
        core = wrapped(me[1] + group % 2, 2)
        return (
            2 * wrapped(me[0] + dx, side_x) + core,
            side_z * wrapped(me[2] + dy, side_y) + wrapped(me[3] + dz, side_z),
        )

    def each_other(first, last, act):
        for group in range(first, last):
            @pl.loop(1 if group == 0 else 0, places)
            def _(place):
                act(group, place)

    def greet(group, place):
        pl.semaphore_signal(barrier, inc=1, device_id=there(group, place), device_id_type=MESH)

    def send(group, place):
        target = there(group, place)
        owner = target[0] * side_y * side_z + target[1]
        for kind, (source, landing) in enumerate(((points, got_points), (chunks, got))):
            pltpu.make_async_remote_copy(
                src_ref=source.at[owner],
                dst_ref=landing.at[group, place],
                send_sem=sent.at[kind],
                recv_sem=got_sems.at[kind, group],
                device_id=target,
                device_id_type=MESH,
            ).start()

    barrier = pltpu.get_barrier_semaphore()
    each_other(0, groups, greet)
    own = src * side_y * side_z + tgt
    pltpu.make_async_copy(points.at[own], got_points.at[0, 0], got_sems.at[0, 0]).start()
    pltpu.make_async_copy(chunks.at[own], got.at[0, 0], got_sems.at[1, 0]).start()
    total[...] = jnp.zeros_like(total)
    pl.semaphore_wait(barrier, count - 1)
    each_other(0, lead, send)
    turned = row_table[...].T
    for kind in range(3):
        for block in range(blocks):
            at = jnp.full((lanes, lanes), kind * blocks + block, jnp.int32)
            row_values[kind, block * lanes : (block + 1) * lanes, :] = jnp.take_along_axis(
                turned, at, axis=1
            )

    def one_group(group, more):
        for kind, landing in enumerate((got_points, got)):
            pltpu.make_async_copy(
                landing.at[group], landing.at[group], got_sems.at[kind, group]
            ).wait()
        pairs = got_points[group].reshape(places, 2 * capacity)
        join = lambda i, at: jnp.concatenate(
            [pairs[i : i + 1, at : at + capacity], pairs[i + 1 : i + 2, at : at + capacity]], axis=1
        )
        col_x = [join(i, 0) for i in range(0, places, 2)]
        col_y = [join(i, capacity) for i in range(0, places, 2)]
        weights = got[group].reshape(columns, width)

        if more:
            for place in range(places):
                send(group + lead, place)
        x, y = row_values[0], row_values[1]
        values = [kernel_values(x, y, a, b) for a, b in zip(col_x, col_y)]
        parts = jnp.concatenate(
            [jnp.concatenate([v[k] for v in values], axis=1) for k in (0, 1)], axis=0
        )
        both = jnp.dot(parts, weights, preferred_element_type=jnp.float32)
        total[0] += both[:rows]
        total[1] += both[rows:]

    @pl.loop(0, groups - lead)
    def _(group):
        one_group(group, True)

    @pl.loop(groups - lead, groups)
    def _(group):
        one_group(group, False)

    half = width // 2
    crossed = total[1] * COSINE[3]
    product = total[0] + jnp.concatenate([-crossed[:, half:], crossed[:, :half]], axis=1)
    out[...] = (product * row_values[2]).astype(jnp.bfloat16)
    for kind, source in enumerate((points, chunks)):
        rest = source.at[pl.ds(0, count - 1)]
        pltpu.make_async_copy(rest, rest, sent.at[kind]).wait()


def sketch_rows(row_first, impedance_rows, chunks, points, mesh_shape, node_count):
    rows = impedance_rows.shape[0]
    count, capacity, width = chunks.shape
    side = math.isqrt(mesh_shape[1])
    sides = (mesh_shape[0] // 2, side, side)
    landing = (2 * side, count // (2 * side))
    turn = node_count / 16.0 / (2.0 * math.pi)
    row_x, row_y = node_points(row_first + jnp.arange(rows, dtype=jnp.int32), node_count)
    scale = impedance_rows / math.sqrt(2.0 * math.pi)
    row_values = (*gridded((row_x * turn, row_y * turn), 0.0), scale)
    table = jnp.concatenate([v.reshape(-1, 128) for v in row_values], axis=0)
    table = jnp.pad(table, ((0, 128 - table.shape[0]), (0, 0)))
    vmem = pl.BlockSpec(memory_space=pltpu.VMEM)
    return pl.pallas_call(
        functools.partial(sketch_kernel, sides, 3),
        out_shape=jax.ShapeDtypeStruct((rows, width), jnp.bfloat16),
        in_specs=[vmem] * 3,
        out_specs=vmem,
        scratch_shapes=[
            pltpu.VMEM((*landing, capacity, width), jnp.bfloat16),
            pltpu.VMEM((*landing, 1, 2 * capacity), jnp.float32),
            pltpu.VMEM((3, rows, 128), jnp.float32),
            pltpu.VMEM((2, rows, width), jnp.float32),
            pltpu.SemaphoreType.DMA((2,)),
            pltpu.SemaphoreType.DMA((2, landing[0])),
        ],
        compiler_params=pltpu.CompilerParams(
            collective_id=1, has_side_effects=True, vmem_limit_bytes=48 << 20
        ),
    )(
        chunks,
        points,
        table,
    )


def split(values, axis, order):
    high = values.astype(jnp.bfloat16)
    rest = values - high.astype(jnp.float32)
    middle = rest.astype(jnp.bfloat16)
    low = (rest - middle.astype(jnp.float32)).astype(jnp.bfloat16)
    pieces = (high, middle, low)
    return jnp.concatenate([pieces[i] for i in order], axis=axis)


LEFT, RIGHT = (0, 0, 1, 0, 1, 2), (0, 1, 0, 2, 1, 0)


def product(first, second, first_axis=1, second_axis=0):
    return lax.dot_general(
        split(first, first_axis, LEFT),
        split(second, second_axis, RIGHT),
        (((first_axis,), (second_axis,)), ((), ())),
        preferred_element_type=jnp.float32,
    )


def spread_rows(row, count):
    return jnp.broadcast_to(row, (count, row.shape[1]))


def eliminate_panel(panel, first, lanes):
    pieces = panel.shape[0] // 8
    rows = [panel[8 * i : 8 * i + 8] for i in range(pieces)]
    sublane = lax.broadcasted_iota(jnp.int32, (8, lanes), 0)
    twice = lambda v: jnp.concatenate([v, v], axis=1)
    done = []
    for top in range(0, pieces, 2):
        columns = [
            {
                i: jnp.take_along_axis(
                    rows[i][:, :lanes],
                    jnp.full((8, lanes), first + 8 * top + t, jnp.int32),
                    axis=1,
                )
                for i in range(top, pieces)
            }
            for t in range(16)
        ]
        for t in range(16):
            here, at = top + t // 8, t % 8
            pivot = spread_rows(columns[t][here][at : at + 1], 8)
            inverse = 1.0 / pivot
            row = rows[here][at : at + 1]
            done.append(row * twice(lax.rsqrt(pivot[0:1])))
            factors = {i: columns[t][i] * inverse for i in range(here, pieces)}
            factors[here] = jnp.where(sublane > at, factors[here], 0.0)
            for u in range(t + 1, 16):
                entry = spread_rows(columns[u][here][at : at + 1], 8)
                for i, f in factors.items():
                    columns[u][i] = columns[u][i] - f * entry
            full_row = spread_rows(row, 8)
            for i, f in factors.items():
                rows[i] = rows[i] - twice(f) * full_row
    return jnp.concatenate(done, axis=0)


def factor_solve(gram_matrix, right):
    size, block = gram_matrix.shape[0], 32
    diagonal = lax.broadcasted_iota(jnp.int32, (size, size), 0) == lax.broadcasted_iota(
        jnp.int32, (size, size), 1
    )
    trace = jnp.sum(jnp.where(diagonal, gram_matrix, 0.0), axis=(0, 1), keepdims=True)
    shifted = gram_matrix + jnp.where(diagonal, 0.25 * trace / size + 1e-06, 0.0)
    rest = jnp.concatenate([shifted, right], axis=1)
    solved = []
    for first in range(0, size, block):
        panel = eliminate_panel(rest[:block], first, size)
        solved.append(panel[:, size:])
        if first + block < size:
            rest = rest[block:] - product(panel[:, :size], panel, 0, 0)[first + block :]
    return jnp.concatenate(solved, axis=0)


def merge_kernel(rows, sketch, maps, out, sends, gots, send_sems, got_sems):
    src, tgt = lax.axis_index("src"), lax.axis_index("tgt")
    mates = (
        tgt + 1 - 2 * (tgt % 2),
        tgt + 2 - 4 * ((tgt // 2) % 2),
        tgt + 3 - 2 * (tgt % 4),
        tgt + 4 - 8 * ((tgt // 4) % 2),
    )
    barrier = pltpu.get_barrier_semaphore()
    for mate in mates:
        pl.semaphore_signal(barrier, inc=1, device_id=(src, mate), device_id_type=MESH)
    copies = []

    def post(values, targets):
        source = sends.at[sum(len(c) > 0 for c in copies)]
        source[...] = values
        base = sum(len(c) for c in copies)
        batch = []
        for i, target in enumerate(targets):
            copy = pltpu.make_async_remote_copy(
                src_ref=source,
                dst_ref=gots.at[base + i],
                send_sem=send_sems.at[base + i],
                recv_sem=got_sems.at[base + i],
                device_id=(src, mates[target]),
                device_id_type=MESH,
            )
            copy.start()
            batch.append((copy, base + i))
        copies.append(batch)
        return batch

    def take(batch):
        values = []
        for copy, slot in batch:
            copy.wait_recv()
            values.append(gots[slot])
        return values

    cross = lax.dot_general(
        sketch[...], sketch[...], (((0,), (0,)), ((), ())), preferred_element_type=jnp.float32
    )
    wide_maps = [maps[k].astype(jnp.float32) for k in range(4)]
    images = [product(cross, m) for m in wide_maps]
    gram_matrix = product(wide_maps[0], images[0], 0, 0) / rows
    turned = factor_solve(gram_matrix, wide_maps[0].T)
    pl.semaphore_wait(barrier, len(mates))
    for level in range(3):
        part = product(turned, images[level + 1]) / (rows * 2**level)
        if level == 0:
            batch = post(part, (0,))
            own = part
        else:
            batch = post(part, (0, 1, 2))
            near, far, beyond = take(batch)
            own = part + near
            if level == 1:
                other = far + beyond
            else:
                own = own + (far + beyond)
                batch = post(own, (3,))
        mine = product(own, own, 0, 0)
        right = product(own, turned, 0, 0)
        if level != 1:
            (other,) = take(batch)
        gram_matrix = (mine + product(other, other, 0, 0)) / 2.0
        turned = factor_solve(gram_matrix, right)
    for batch in copies:
        for copy, _ in batch:
            copy.wait_send()
    out[...] = split(turned, 1, (0, 1, 2))


def bases_kernel(sketch, turned, out):
    out[...] = lax.dot_general(
        jnp.concatenate([sketch[...]] * 3, axis=1),
        turned[...],
        (((1,), (1,)), ((), ())),
        preferred_element_type=jnp.float32,
    )


def merged_bases(sketch, maps_here):
    rows, width = sketch.shape
    tile = (width, width)
    turned = pl.pallas_call(
        functools.partial(merge_kernel, rows),
        out_shape=jax.ShapeDtypeStruct((width, 3 * width), jnp.bfloat16),
        in_specs=[pl.BlockSpec(memory_space=pltpu.VMEM)] * 2,
        out_specs=pl.BlockSpec(memory_space=pltpu.VMEM),
        scratch_shapes=[
            pltpu.VMEM((4, *tile), jnp.float32),
            pltpu.VMEM((8, *tile), jnp.float32),
            pltpu.SemaphoreType.DMA((8,)),
            pltpu.SemaphoreType.DMA((8,)),
        ],
        compiler_params=pltpu.CompilerParams(
            collective_id=0, has_side_effects=True, vmem_limit_bytes=40 << 20
        ),
    )(sketch, maps_here)
    row_spec = pl.BlockSpec((rows // 2, width), lambda i: (i, 0))
    return pl.pallas_call(
        bases_kernel,
        grid=(2,),
        out_shape=jax.ShapeDtypeStruct((rows, width), jnp.float32),
        in_specs=[row_spec, pl.BlockSpec((width, 3 * width), lambda i: (0, 0))],
        out_specs=row_spec,
        compiler_params=pltpu.CompilerParams(vmem_limit_bytes=16 << 20),
    )(sketch, turned)


def sketch_of(omega, owners, columns, impedance):
    mesh_shape = (lax.axis_size("src"), lax.axis_size("tgt"))
    rows = impedance.shape[0]
    node_count = mesh_shape[1] * rows
    count = mesh_shape[0] * mesh_shape[1]
    chunks, points = packed_chunks(omega, owners, columns, count, node_count)
    chunks = chunks.reshape(count, -1, chunks.shape[1])
    points = points.reshape(count, 1, -1)
    first = lax.axis_index("tgt") * rows
    return sketch_rows(first, impedance, chunks, points, mesh_shape, node_count)


def per_device(omega, owners, columns, impedance, level_maps):
    return merged_bases(sketch_of(omega, owners, columns, impedance), level_maps[0])[None]


def solution(mesh):
    in_specs = (
        P(("src", "tgt"), None),
        P(("src", "tgt"), None),
        P(("src", "tgt")),
        P("tgt"),
        P("src", None, None, None),
    )
    out_specs = P("src", "tgt", None)
    return jax.shard_map(
        per_device, mesh=mesh, in_specs=in_specs, out_specs=out_specs, check_vma=False
    )
```

```python
import functools
import math

import jax
import jax.numpy as jnp
from jax import lax
from jax.experimental import pallas as pl
from jax.experimental.pallas import tpu as pltpu
from jax.sharding import PartitionSpec as P

MESH = pl.DeviceIdType.MESH
SINE = (4.4415356787207045, -7.2646801556685014, 3.252047353220934)
COSINE = (1.414204078817102, -6.977641981219209, 5.715237646584958, -1.728346667500456)


def node_points(node_index, node_count):
    angles = 2.0 * math.pi / node_count * (node_index.astype(jnp.float32) + 0.5)
    radius = 1.0 + 0.25 * jnp.cos(3.0 * angles)
    return (radius * jnp.cos(angles), radius * jnp.sin(angles))


def pack_kernel(
    capacity,
    node_count,
    codes,
    omega,
    chunks_out,
    points_out,
    places,
    placed,
    table,
    wide,
    plain,
    sem,
):
    blocks, lanes = codes.shape
    count = points_out.shape[0]
    owner_at = lax.broadcasted_iota(jnp.int32, (count, lanes), 0)
    before = (
        lax.broadcasted_iota(jnp.int32, (lanes, lanes), 0)
        < lax.broadcasted_iota(jnp.int32, (lanes, lanes), 1)
    ).astype(jnp.float32)
    counted = jnp.concatenate([before, jnp.ones_like(before)], axis=1).astype(jnp.bfloat16)
    rank_at = lax.broadcasted_iota(jnp.int32, (capacity, lanes), 0)
    wide[...] = jnp.zeros_like(wide)
    table[...] = jnp.zeros_like(table)
    plain[...] = omega[...].astype(jnp.float32)

    def one_block(index, running):
        here = pl.ds(index, 1)
        code = codes[here, :]
        owner, column = code >> 15, code & 32767
        named = owner_at == owner
        onehot = named.astype(jnp.float32).astype(jnp.bfloat16)
        counts = jnp.dot(onehot, counted, preferred_element_type=jnp.float32)
        earlier = counts[:, :lanes] + running
        rank = jnp.sum(jnp.where(named, earlier, 0.0), axis=0, keepdims=True).astype(jnp.int32)
        places[here, :] = owner * capacity + rank
        ranked = rank_at == rank
        digits = [
            jnp.where(ranked, digit.astype(jnp.float32), 0.0).astype(jnp.bfloat16)
            for digit in (column // 256, column % 256)
        ]
        table[...] += lax.dot_general(
            onehot,
            jnp.concatenate(digits, axis=0),
            (((1,), (1,)), ((), ())),
            preferred_element_type=jnp.float32,
        )
        return running + counts[:, lanes:]

    lax.fori_loop(0, blocks, one_block, jnp.zeros((count, lanes), jnp.float32), unroll=8)
    copy = pltpu.make_async_copy(places, placed, sem)
    copy.start()
    digits = table[...]
    column = digits[:, :capacity] * 256.0 + digits[:, capacity:]
    turn = node_count / 16.0 / (2.0 * math.pi)
    point_x, point_y = node_points(column, node_count)
    points_out[...] = jnp.concatenate(gridded((point_x * turn, point_y * turn), 0.5), axis=1)
    copy.wait()

    @pl.loop(0, blocks)
    def _(block):
        for first in range(0, lanes, 8):
            rows = plain[pl.ds(pl.multiple_of(block * lanes + first, 8), 8), :]
            for i in range(8):
                wide[pl.ds(placed[block, first + i], 1), :] = rows[i : i + 1]

    chunks_out[...] = wide[...].astype(jnp.bfloat16)


def packed_chunks(omega, owners, columns, count, node_count):
    samples, width = omega.shape
    lanes = 128
    blocks = samples // lanes
    capacity = 2 * samples // count
    codes = owners.reshape(blocks, lanes) * 32768 + columns.reshape(blocks, lanes)
    vmem = pl.BlockSpec(memory_space=pltpu.VMEM)
    return pl.pallas_call(
        functools.partial(pack_kernel, capacity, node_count),
        out_shape=(
            jax.ShapeDtypeStruct((count * capacity, width), jnp.bfloat16),
            jax.ShapeDtypeStruct((count, 2 * capacity), jnp.float32),
        ),
        in_specs=[vmem] * 2,
        out_specs=(vmem, vmem),
        scratch_shapes=[
            pltpu.VMEM((blocks, lanes), jnp.int32),
            pltpu.SMEM((blocks, lanes), jnp.int32),
            pltpu.VMEM((count, 2 * capacity), jnp.float32),
            pltpu.VMEM((count * capacity, width), jnp.float32),
            pltpu.VMEM((samples, width), jnp.float32),
            pltpu.SemaphoreType.DMA,
        ],
        compiler_params=pltpu.CompilerParams(vmem_limit_bytes=40 << 20),
    )(codes, omega)


def gridded(points, shift):
    x, y = points
    return (jnp.floor(x * 16384.0 + (0.5 - shift)) + shift) / 16384.0, y


def kernel_values(x, y, col_x, col_y):
    dx = x - col_x
    dy = y - col_y
    square = dx * dx + dy * dy
    turns = square * lax.rsqrt(square)
    part = turns - jnp.round(turns)
    amplitude = lax.rsqrt(turns + 0.5 / math.pi)
    z = part * part
    sine = part * (SINE[0] + z * (SINE[1] + z * SINE[2]))
    cosine = COSINE[0] / COSINE[3] + z * (COSINE[1] / COSINE[3] + z * (COSINE[2] / COSINE[3] + z))
    scaled = amplitude * sine
    return (amplitude - scaled * sine).astype(jnp.bfloat16), (scaled * cosine).astype(jnp.bfloat16)


def sketch_kernel(
    sides,
    lead,
    chunks,
    points,
    row_table,
    out,
    got,
    got_points,
    row_values,
    total,
    sent,
    got_sems,
):
    src, tgt = lax.axis_index("src"), lax.axis_index("tgt")
    rows, lanes = total.shape[1:]
    count, capacity, width = chunks.shape
    groups, places = got.shape[:2]
    side_x, side_y, side_z = sides
    columns = places * capacity
    blocks = rows // lanes
    me = (src // 2, src % 2, tgt // side_z, tgt % side_z)

    def wrapped(index, size):
        return jnp.where(index >= size, index - size, index)

    def there(group, place):
        dx, dy, dz = place // side_y, place % side_y, group // 2
        for back in (dx, dy):
            dz = jnp.where(dz < back, dz + side_z - back, dz - back)
        core = wrapped(me[1] + group % 2, 2)
        return (
            2 * wrapped(me[0] + dx, side_x) + core,
            side_z * wrapped(me[2] + dy, side_y) + wrapped(me[3] + dz, side_z),
        )

    def each_other(first, last, act):
        for group in range(first, last):
            @pl.loop(1 if group == 0 else 0, places)
            def _(place):
                act(group, place)

    def greet(group, place):
        pl.semaphore_signal(barrier, inc=1, device_id=there(group, place), device_id_type=MESH)

    def send(group, place):
        target = there(group, place)
        owner = target[0] * side_y * side_z + target[1]
        for kind, (source, landing) in enumerate(((points, got_points), (chunks, got))):
            pltpu.make_async_remote_copy(
                src_ref=source.at[owner],
                dst_ref=landing.at[group, place],
                send_sem=sent.at[kind],
                recv_sem=got_sems.at[kind, group],
                device_id=target,
                device_id_type=MESH,
            ).start()

    barrier = pltpu.get_barrier_semaphore()
    each_other(0, groups, greet)
    own = src * side_y * side_z + tgt
    pltpu.make_async_copy(points.at[own], got_points.at[0, 0], got_sems.at[0, 0]).start()
    pltpu.make_async_copy(chunks.at[own], got.at[0, 0], got_sems.at[1, 0]).start()
    total[...] = jnp.zeros_like(total)
    pl.semaphore_wait(barrier, count - 1)
    each_other(0, lead, send)
    turned = row_table[...].T
    for kind in range(3):
        for block in range(blocks):
            at = jnp.full((lanes, lanes), kind * blocks + block, jnp.int32)
            row_values[kind, block * lanes : (block + 1) * lanes, :] = jnp.take_along_axis(
                turned, at, axis=1
            )

    def one_group(group, more):
        for kind, landing in enumerate((got_points, got)):
            pltpu.make_async_copy(
                landing.at[group], landing.at[group], got_sems.at[kind, group]
            ).wait()
        pairs = got_points[group].reshape(places, 2 * capacity)
        join = lambda i, at: jnp.concatenate(
            [pairs[i : i + 1, at : at + capacity], pairs[i + 1 : i + 2, at : at + capacity]], axis=1
        )
        col_x = [join(i, 0) for i in range(0, places, 2)]
        col_y = [join(i, capacity) for i in range(0, places, 2)]
        weights = got[group].reshape(columns, width)

        if more:
            for place in range(places):
                send(group + lead, place)
        x, y = row_values[0], row_values[1]
        values = [kernel_values(x, y, a, b) for a, b in zip(col_x, col_y)]
        parts = jnp.concatenate(
            [jnp.concatenate([v[k] for v in values], axis=1) for k in (0, 1)], axis=0
        )
        both = jnp.dot(parts, weights, preferred_element_type=jnp.float32)
        total[0] += both[:rows]
        total[1] += both[rows:]

    @pl.loop(0, groups - lead)
    def _(group):
        one_group(group, True)

    @pl.loop(groups - lead, groups)
    def _(group):
        one_group(group, False)

    half = width // 2
    crossed = total[1] * COSINE[3]
    product = total[0] + jnp.concatenate([-crossed[:, half:], crossed[:, :half]], axis=1)
    out[...] = (product * row_values[2]).astype(jnp.bfloat16)
    for kind, source in enumerate((points, chunks)):
        rest = source.at[pl.ds(0, count - 1)]
        pltpu.make_async_copy(rest, rest, sent.at[kind]).wait()


def sketch_rows(row_first, impedance_rows, chunks, points, mesh_shape, node_count):
    rows = impedance_rows.shape[0]
    count, capacity, width = chunks.shape
    side = math.isqrt(mesh_shape[1])
    sides = (mesh_shape[0] // 2, side, side)
    landing = (2 * side, count // (2 * side))
    turn = node_count / 16.0 / (2.0 * math.pi)
    row_x, row_y = node_points(row_first + jnp.arange(rows, dtype=jnp.int32), node_count)
    scale = impedance_rows / math.sqrt(2.0 * math.pi)
    row_values = (*gridded((row_x * turn, row_y * turn), 0.0), scale)
    table = jnp.concatenate([v.reshape(-1, 128) for v in row_values], axis=0)
    table = jnp.pad(table, ((0, 128 - table.shape[0]), (0, 0)))
    vmem = pl.BlockSpec(memory_space=pltpu.VMEM)
    return pl.pallas_call(
        functools.partial(sketch_kernel, sides, 3),
        out_shape=jax.ShapeDtypeStruct((rows, width), jnp.bfloat16),
        in_specs=[vmem] * 3,
        out_specs=vmem,
        scratch_shapes=[
            pltpu.VMEM((*landing, capacity, width), jnp.bfloat16),
            pltpu.VMEM((*landing, 1, 2 * capacity), jnp.float32),
            pltpu.VMEM((3, rows, 128), jnp.float32),
            pltpu.VMEM((2, rows, width), jnp.float32),
            pltpu.SemaphoreType.DMA((2,)),
            pltpu.SemaphoreType.DMA((2, landing[0])),
        ],
        compiler_params=pltpu.CompilerParams(
            collective_id=1, has_side_effects=True, vmem_limit_bytes=48 << 20
        ),
    )(
        chunks,
        points,
        table,
    )


def split(values, axis, order):
    high = values.astype(jnp.bfloat16)
    rest = values - high.astype(jnp.float32)
    middle = rest.astype(jnp.bfloat16)
    low = (rest - middle.astype(jnp.float32)).astype(jnp.bfloat16)
    pieces = (high, middle, low)
    return jnp.concatenate([pieces[i] for i in order], axis=axis)


LEFT, RIGHT = (0, 0, 1, 0, 1, 2), (0, 1, 0, 2, 1, 0)


def product(first, second, first_axis=1, second_axis=0):
    return lax.dot_general(
        split(first, first_axis, LEFT),
        split(second, second_axis, RIGHT),
        (((first_axis,), (second_axis,)), ((), ())),
        preferred_element_type=jnp.float32,
    )


def spread_rows(row, count):
    return jnp.broadcast_to(row, (count, row.shape[1]))


def eliminate_panel(panel, first, lanes):
    pieces = panel.shape[0] // 8
    rows = [panel[8 * i : 8 * i + 8] for i in range(pieces)]
    sublane = lax.broadcasted_iota(jnp.int32, (8, lanes), 0)
    twice = lambda v: jnp.concatenate([v, v], axis=1)
    done = []
    for top in range(0, pieces, 2):
        columns = [
            {
                i: jnp.take_along_axis(
                    rows[i][:, :lanes],
                    jnp.full((8, lanes), first + 8 * top + t, jnp.int32),
                    axis=1,
                )
                for i in range(top, pieces)
            }
            for t in range(16)
        ]
        for t in range(16):
            here, at = top + t // 8, t % 8
            pivot = spread_rows(columns[t][here][at : at + 1], 8)
            inverse = 1.0 / pivot
            row = rows[here][at : at + 1]
            done.append(row * twice(lax.rsqrt(pivot[0:1])))
            factors = {i: columns[t][i] * inverse for i in range(here, pieces)}
            factors[here] = jnp.where(sublane > at, factors[here], 0.0)
            for u in range(t + 1, 16):
                entry = spread_rows(columns[u][here][at : at + 1], 8)
                for i, f in factors.items():
                    columns[u][i] = columns[u][i] - f * entry
            full_row = spread_rows(row, 8)
            for i, f in factors.items():
                rows[i] = rows[i] - twice(f) * full_row
    return jnp.concatenate(done, axis=0)


def factor_solve(gram_matrix, right):
    size, block = gram_matrix.shape[0], 32
    diagonal = lax.broadcasted_iota(jnp.int32, (size, size), 0) == lax.broadcasted_iota(
        jnp.int32, (size, size), 1
    )
    trace = jnp.sum(jnp.where(diagonal, gram_matrix, 0.0), axis=(0, 1), keepdims=True)
    shifted = gram_matrix + jnp.where(diagonal, 0.25 * trace / size + 1e-06, 0.0)
    rest = jnp.concatenate([shifted, right], axis=1)
    solved = []
    for first in range(0, size, block):
        panel = eliminate_panel(rest[:block], first, size)
        solved.append(panel[:, size:])
        if first + block < size:
            rest = rest[block:] - product(panel[:, :size], panel, 0, 0)[first + block :]
    return jnp.concatenate(solved, axis=0)


def merge_kernel(rows, sketch, maps, out, sends, gots, send_sems, got_sems):
    src, tgt = lax.axis_index("src"), lax.axis_index("tgt")
    mates = (
        tgt + 1 - 2 * (tgt % 2),
        tgt + 2 - 4 * ((tgt // 2) % 2),
        tgt + 3 - 2 * (tgt % 4),
        tgt + 4 - 8 * ((tgt // 4) % 2),
    )
    barrier = pltpu.get_barrier_semaphore()
    for mate in mates:
        pl.semaphore_signal(barrier, inc=1, device_id=(src, mate), device_id_type=MESH)
    copies = []

    def post(values, targets):
        source = sends.at[sum(len(c) > 0 for c in copies)]
        source[...] = values
        base = sum(len(c) for c in copies)
        batch = []
        for i, target in enumerate(targets):
            copy = pltpu.make_async_remote_copy(
                src_ref=source,
                dst_ref=gots.at[base + i],
                send_sem=send_sems.at[base + i],
                recv_sem=got_sems.at[base + i],
                device_id=(src, mates[target]),
                device_id_type=MESH,
            )
            copy.start()
            batch.append((copy, base + i))
        copies.append(batch)
        return batch

    def take(batch):
        values = []
        for copy, slot in batch:
            copy.wait_recv()
            values.append(gots[slot])
        return values

    cross = lax.dot_general(
        sketch[...], sketch[...], (((0,), (0,)), ((), ())), preferred_element_type=jnp.float32
    )
    wide_maps = [maps[k].astype(jnp.float32) for k in range(4)]
    images = [product(cross, m) for m in wide_maps]
    gram_matrix = product(wide_maps[0], images[0], 0, 0) / rows
    turned = factor_solve(gram_matrix, wide_maps[0].T)
    pl.semaphore_wait(barrier, len(mates))
    for level in range(3):
        part = product(turned, images[level + 1]) / (rows * 2**level)
        if level == 0:
            batch = post(part, (0,))
            own = part
        else:
            batch = post(part, (0, 1, 2))
            near, far, beyond = take(batch)
            own = part + near
            if level == 1:
                other = far + beyond
            else:
                own = own + (far + beyond)
                batch = post(own, (3,))
        mine = product(own, own, 0, 0)
        right = product(own, turned, 0, 0)
        if level != 1:
            (other,) = take(batch)
        gram_matrix = (mine + product(other, other, 0, 0)) / 2.0
        turned = factor_solve(gram_matrix, right)
    for batch in copies:
        for copy, _ in batch:
            copy.wait_send()
    out[...] = split(turned, 1, (0, 1, 2))


def bases_kernel(sketch, turned, out):
    out[...] = lax.dot_general(
        jnp.concatenate([sketch[...]] * 3, axis=1),
        turned[...],
        (((1,), (1,)), ((), ())),
        preferred_element_type=jnp.float32,
    )


def merged_bases(sketch, maps_here):
    rows, width = sketch.shape
    tile = (width, width)
    turned = pl.pallas_call(
        functools.partial(merge_kernel, rows),
        out_shape=jax.ShapeDtypeStruct((width, 3 * width), jnp.bfloat16),
        in_specs=[pl.BlockSpec(memory_space=pltpu.VMEM)] * 2,
        out_specs=pl.BlockSpec(memory_space=pltpu.VMEM),
        scratch_shapes=[
            pltpu.VMEM((4, *tile), jnp.float32),
            pltpu.VMEM((8, *tile), jnp.float32),
            pltpu.SemaphoreType.DMA((8,)),
            pltpu.SemaphoreType.DMA((8,)),
        ],
        compiler_params=pltpu.CompilerParams(
            collective_id=0, has_side_effects=True, vmem_limit_bytes=40 << 20
        ),
    )(sketch, maps_here)
    row_spec = pl.BlockSpec((rows // 2, width), lambda i: (i, 0))
    return pl.pallas_call(
        bases_kernel,
        grid=(2,),
        out_shape=jax.ShapeDtypeStruct((rows, width), jnp.float32),
        in_specs=[row_spec, pl.BlockSpec((width, 3 * width), lambda i: (0, 0))],
        out_specs=row_spec,
        compiler_params=pltpu.CompilerParams(vmem_limit_bytes=16 << 20),
    )(sketch, turned)


def sketch_of(omega, owners, columns, impedance):
    mesh_shape = (lax.axis_size("src"), lax.axis_size("tgt"))
    rows = impedance.shape[0]
    node_count = mesh_shape[1] * rows
    count = mesh_shape[0] * mesh_shape[1]
    chunks, points = packed_chunks(omega, owners, columns, count, node_count)
    chunks = chunks.reshape(count, -1, chunks.shape[1])
    points = points.reshape(count, 1, -1)
    first = lax.axis_index("tgt") * rows
    return sketch_rows(first, impedance, chunks, points, mesh_shape, node_count)


def per_device(omega, owners, columns, impedance, level_maps):
    return merged_bases(sketch_of(omega, owners, columns, impedance), level_maps[0])[None]


def solution(mesh):
    in_specs = (
        P(("src", "tgt"), None),
        P(("src", "tgt"), None),
        P(("src", "tgt")),
        P("tgt"),
        P("src", None, None, None),
    )
    out_specs = P("src", "tgt", None)
    return jax.shard_map(
        per_device, mesh=mesh, in_specs=in_specs, out_specs=out_specs, check_vma=False
    )
```
